256 devices in a mesh: seq: 16 (over x_hi, z), chan: 8 (over x_lo, y), dp: 2 (over core).
Axes of the slice: x: 4 (x_hi: 2, x_lo: 2; x = x_hi * 2 + x_lo), y: 4, z: 8, core: 2. Of those that a mesh axis runs over, the one named last changes fastest.
Arguments:
- query_proj: float32 [4096, 4096], P(('dp', 'seq'), 'chan'), parts along dimension 0, may hold values from -6 to 6
- key_proj: float32 [4096, 4096], P(('dp', 'seq'), 'chan'), parts along dimension 0, may hold values from -6 to 6
- value_proj: float32 [4096, 4096], P(('dp', 'seq'), 'chan'), parts along dimension 0, may hold values from -6 to 6
- filter_taps: float32 [2048, 4096], P('seq', 'chan'), may hold values from -6 to 6
- skip_gain: float32 [4096], P('chan'), may hold values from 0.25 to 2
- out_grad: float32 [4096, 4096], P(('dp', 'seq'), 'chan'), parts along dimension 0, may hold values from -6 to 6
- block_order: int32 [32], P('dp'), parts along dimension 0, may hold values from 0 to 15, each once
Outputs:
- hyena_out: bfloat16 [4096, 4096], P(('dp', 'seq'), 'chan'), parts along dimension 0
- grad_query: bfloat16 [4096, 4096], P(('dp', 'seq'), 'chan'), parts along dimension 0
- grad_key: bfloat16 [4096, 4096], P(('dp', 'seq'), 'chan'), parts along dimension 0
- grad_value: bfloat16 [4096, 4096], P(('dp', 'seq'), 'chan'), parts along dimension 0
- grad_filter: bfloat16 [4096, 4096], P(('dp', 'seq'), 'chan'), parts along dimension 0
The draws below stay inside these ranges and needn't reach their ends.
There are 2 independent parts, one for each index of `dp`. The reference program is written for one: setup_inputs(seed, part) draws one part's arguments, and reference() takes and returns one part's arrays. A program takes and returns all parts, laid end to end along the dimension named above; an argument that names none is the same for every part. Nothing has to cross between parts.
Inputs may be any that keep to these rules, and one draw needn't show every extreme that they name: `block_order`: each loop position holds a different sequence block; every block index appears once.
All inputs are finite; a program needn't handle non-finite values.
Results may differ from the reference program's by a relative error of at most 0.0075.
Values may be sent and summed in bfloat16 or wider, within the bound.
A program may use at most 64 MiB of HBM per device.

```python
import math
import jax
import jax.numpy as jnp
from jax import lax

D = 4096
TOK_DEV = 128
TOKENS = 2048
N_SEQ = 16


def block_levels(stream_key, extent, shards, low, largest):
    def one(position, blocks):
        heights = jax.random.uniform(jax.random.fold_in(jax.random.fold_in(stream_key, 6), position), (blocks,), jnp.float32, low / len(shards), largest / len(shards))
        return jnp.repeat(jnp.exp(heights), extent[position] // blocks).reshape((-1,) + (1,) * (len(extent) - position - 1))

    loudness = one(*shards[0])
    for cut in shards[1:]:
        loudness = loudness * one(*cut)
    return loudness


def scatter_about(key, extent, scale, most, shards=(), kind=jnp.bfloat16):
    drawn = jax.random.normal(key, extent, jnp.float32) * scale
    if len(shards) > 0:
        drawn = block_levels(key, extent, shards, -0.22, 0.18) * drawn
    return jnp.clip(drawn, min=-most, max=most).astype(kind)


def setup_inputs(seed: int = 0, part: int = 0) -> dict:
    streams_of = jax.random.split(jax.random.key(seed), 8)
    own_keys = jax.random.split(jax.random.fold_in(streams_of[7], part), 8)
    return {
        "query_proj": scatter_about(own_keys[0], (TOKENS, D), 1.0, 6.0, ((0, 16), (1, 8)), jnp.float32),
        "key_proj": scatter_about(own_keys[1], (TOKENS, D), 1.0, 6.0, ((0, 16), (1, 8)), jnp.float32),
        "value_proj": scatter_about(own_keys[2], (TOKENS, D), 1.0, 6.0, ((0, 16), (1, 8)), jnp.float32),
        "filter_taps": scatter_about(streams_of[3], (TOKENS, D), 1.0, 6.0, ((0, 16), (1, 8)), jnp.float32),
        "skip_gain": jnp.clip(jnp.exp(math.log(2.0) - 2.0794415 * jax.random.uniform(streams_of[4], (D,), jnp.float32) ** block_levels(streams_of[4], (D,), ((0, 8),), -0.2, 0.2)), 0.25, 2.0),
        "out_grad": scatter_about(own_keys[5], (TOKENS, D), 1.0, 6.0, ((0, 16), (1, 8)), jnp.float32),
        "block_order": jax.random.permutation(own_keys[6], N_SEQ).astype(jnp.int32),
    }


def transform_table(spectrum_length, input_length):
    frequency = lax.broadcasted_iota(jnp.float32, (spectrum_length, input_length), 0)
    time_index = lax.broadcasted_iota(jnp.float32, (spectrum_length, input_length), 1)
    angles = 2.0 * math.pi / spectrum_length * jnp.mod(frequency * time_index, spectrum_length)
    return jnp.concatenate([jnp.cos(angles), -jnp.sin(angles)], axis=0).astype(jnp.bfloat16)

def inverse_table(points, spectrum_length):
    frequency = lax.broadcasted_iota(jnp.float32, (points.shape[0], spectrum_length), 1)
    angles = 2.0 * math.pi / spectrum_length * jnp.mod(points[:, None] * frequency, spectrum_length)
    table_values = jnp.concatenate([jnp.cos(angles), -jnp.sin(angles)], axis=1) / spectrum_length
    return table_values.astype(jnp.bfloat16)

def complex_mul(first_spec, second_spec):
    half_len = first_spec.shape[-2] // 2
    first_re = first_spec[..., :half_len, :]
    first_im = first_spec[..., half_len:, :]
    second_re = second_spec[..., :half_len, :]
    second_im = second_spec[..., half_len:, :]
    return jnp.concatenate([first_re * second_re - first_im * second_im, first_re * second_im + first_im * second_re], axis=-2)

def conjugate(spectrum):
    half_len = spectrum.shape[-2] // 2
    return jnp.concatenate([spectrum[..., :half_len, :], -spectrum[..., half_len:, :]], axis=-2)

def alternating(spectrum_length):
    frequency = lax.broadcasted_iota(jnp.float32, (spectrum_length, 1), 0)
    sign_half = 1.0 - 2.0 * jnp.mod(frequency, 2.0)
    return jnp.concatenate([sign_half, sign_half], axis=0)

def bf16_round(values):
    return lax.optimization_barrier(values.astype(jnp.bfloat16)).astype(jnp.float32)

def reference(query_proj, key_proj, value_proj, filter_taps, skip_gain, out_grad, block_order):
    loop_size = N_SEQ
    block_rows = TOK_DEV
    channels = D
    spectrum_length = 2 * block_rows
    tap_scale = 1.0 / math.sqrt(block_rows * loop_size)
    highest = lax.Precision.HIGHEST
    mixed = (key_proj * value_proj).astype(jnp.bfloat16)
    gated = (out_grad * query_proj).astype(jnp.bfloat16)
    scaled_taps = (filter_taps * tap_scale).astype(jnp.bfloat16)
    half_table = transform_table(spectrum_length, block_rows).astype(jnp.float32)
    full_table = transform_table(spectrum_length, spectrum_length).astype(jnp.float32)
    row_points = lax.broadcasted_iota(jnp.float32, (block_rows,), 0)
    output_table = inverse_table(row_points + block_rows, spectrum_length).astype(jnp.float32)
    gradient_table = inverse_table(block_rows - row_points, spectrum_length).astype(jnp.float32)
    taps_table = inverse_table(lax.broadcasted_iota(jnp.float32, (spectrum_length,), 0), spectrum_length).astype(jnp.float32)
    sign_column = alternating(spectrum_length)
    positions = jnp.arange(loop_size, dtype=jnp.int32)
    holder = lax.optimization_barrier(jnp.sum(jnp.where(block_order[None, :] == positions[:, None], positions[None, :], 0), axis=1)).astype(jnp.int32)
    mixed_seq = jnp.take(mixed.reshape(loop_size, block_rows, channels), holder, axis=0).astype(jnp.float32)
    gated_seq = jnp.take(gated.reshape(loop_size, block_rows, channels), holder, axis=0).astype(jnp.float32)
    mixed_spec = jnp.einsum('mt,ntc->nmc', half_table, mixed_seq, precision=highest)
    gated_spec = jnp.einsum('mt,ntc->nmc', half_table, gated_seq, precision=highest)
    signed_gated = sign_column * gated_spec
    padded_taps = jnp.concatenate([jnp.zeros((block_rows, channels), jnp.float32), scaled_taps.astype(jnp.float32)], axis=0)
    out_spec = jnp.zeros((loop_size, 2 * spectrum_length, channels), jnp.float32)
    grad_spec = jnp.zeros((loop_size, 2 * spectrum_length, channels), jnp.float32)
    partial_value = jnp.zeros(((loop_size + 1) * block_rows, channels), jnp.float32)
    for lag_index in range(loop_size):
        offset = lag_index * block_rows
        response = jnp.dot(full_table, padded_taps[offset:offset + spectrum_length], precision=highest)
        count = loop_size - lag_index
        earlier = mixed_spec[:count]
        later_spec = gated_spec[lag_index:]
        out_spec = out_spec.at[lag_index:].add(complex_mul(earlier, response))
        grad_spec = grad_spec.at[:count].add(complex_mul(conjugate(later_spec), response))
        product = bf16_round(complex_mul(conjugate(earlier), signed_gated[lag_index:]))
        lag_taps = jnp.dot(taps_table, lax.optimization_barrier(jnp.sum(product, axis=0)), precision=highest)
        partial_value = partial_value.at[offset:offset + spectrum_length].add(lag_taps)
    gain_row = skip_gain.astype(jnp.float32)[None, None, :]
    conv_seq = jnp.einsum('tm,nmc->ntc', output_table, bf16_round(out_spec), precision=highest) + gain_row * mixed_seq
    grad_seq = jnp.einsum('tm,nmc->ntc', gradient_table, bf16_round(grad_spec), precision=highest) + gain_row * gated_seq
    conv_out = jnp.take(conv_seq, block_order, axis=0).reshape(loop_size * block_rows, channels)
    conv_grad = jnp.take(grad_seq, block_order, axis=0).reshape(loop_size * block_rows, channels)
    hyena_out = (query_proj * conv_out).astype(jnp.bfloat16)
    grad_query = (out_grad * conv_out).astype(jnp.bfloat16)
    grad_key = (conv_grad * value_proj).astype(jnp.bfloat16)
    grad_value = (conv_grad * key_proj).astype(jnp.bfloat16)
    grad_filter = (partial_value[block_rows:] * tap_scale).astype(jnp.bfloat16)
    return (hyena_out, grad_query, grad_key, grad_value, grad_filter)
```

```python
import functools
import math

import jax
import jax.numpy as jnp
import ml_dtypes
import numpy as np
from jax import lax
from jax.experimental import pallas as pl
from jax.experimental.pallas import tpu as pltpu
from jax.sharding import PartitionSpec as P

MESH = pl.DeviceIdType.MESH
HALVES = 2


def spectrum_tables(rows):
    length = 2 * rows
    time = np.arange(rows)[:, None]
    freq = np.arange(rows)[None, :]
    angle = 2.0 * np.pi / length * ((time * freq) % length)
    middle = 1.0 - 2.0 * (time % 2)
    sine = np.where(freq == 0, middle, -np.sin(angle))
    forward = np.concatenate([np.cos(angle), sine], axis=1)
    sign = 1.0 - 2.0 * (freq % 2)
    weight = np.where(freq == 0, 1.0, 2.0) / length
    output = np.concatenate([weight * sign * np.cos(angle), weight * sign * sine], axis=1).T
    lag_sine = np.where(freq == 0, middle, np.sin(angle))
    lags = np.concatenate([weight * np.cos(angle), weight * lag_sine], axis=1).T
    return [t.astype(ml_dtypes.bfloat16) for t in (forward, output, lags)]


def kernel(
    n, q_ref, k_ref, v_ref, o_ref, taps_ref, gain_ref, order_ref, fwd_ref, out_tab_ref, lag_tab_ref,
    hyena_ref, gq_ref, gk_ref, gv_ref, gf_ref,
    send_in, recv_a, recv_b, send_out, back, mixed_s, gated_s, resp_s, sum_s, sum_g, sum_f,
    send_sem, recv_sem, back_send, back_recv,
):
    me = lax.axis_index("seq")
    rows, channels = q_ref.shape
    own = channels // n
    part = own // HALVES
    scale = 1.0 / math.sqrt(rows * n)
    bf16, f32 = jnp.bfloat16, jnp.float32

    barrier = pltpu.get_barrier_semaphore()
    for step in range(1, n):
        pl.semaphore_signal(barrier, inc=1, device_id={"seq": lax.rem(me + step, n)}, device_id_type=MESH)

    for a in range(3):
        for g in range(channels // 128):
            cols = slice(g * 128, (g + 1) * 128)
            if a == 0:
                block = k_ref[:, cols] * v_ref[:, cols]
            elif a == 1:
                block = o_ref[:, cols] * q_ref[:, cols]
            else:
                block = taps_ref[:, cols] * scale
            turned = block.T.astype(bf16)
            for i in range(128 // part):
                peer, half = (g * 128 + i * part) // own, i % HALVES
                send_in[half, peer, a * part:(a + 1) * part, :] = turned[i * part:(i + 1) * part]

    pl.semaphore_wait(barrier, n - 1)

    recvs = (recv_a, recv_b)
    hops = [(h, z) for z in (4, 3, 5, 2, 6, 1, 7, 0) for h in (1, 0) if (h, z) != (0, 0)]

    def peer_of(hop):
        h, z = hop
        ring = n // 2
        return lax.rem(me // ring + h, 2) * ring + lax.rem(me + z, ring)

    for half in range(HALVES):
        for hop in hops:
            peer = peer_of(hop)
            pltpu.make_async_remote_copy(
                src_ref=send_in.at[half, peer], dst_ref=recvs[half].at[me],
                send_sem=send_sem, recv_sem=recv_sem.at[half],
                device_id={"seq": peer}, device_id_type=MESH,
            ).start()
    for half in range(HALVES):
        recvs[half][me] = send_in[half, me]

    order = [order_ref[p] for p in range(n)]
    holder = []
    for j in range(n):
        at = jnp.int32(0)
        for p in range(1, n):
            at = jnp.where(order[p] == j, p, at)
        holder.append(at)

    lane = lax.broadcasted_iota(jnp.int32, (8, 128), 1)
    first = lane == 0
    sign = jnp.where(lane % 2 == 0, 1.0, -1.0).astype(f32)
    wide_lane = lax.broadcasted_iota(jnp.int32, (n * part, 2 * rows), 1)
    wide_sign = jnp.where(wide_lane % 2 == 0, 1.0, -1.0).astype(f32)
    re, im = slice(0, 128), slice(128, 256)

    for half in range(HALVES):
        recv = recvs[half]
        landed = recv.at[pl.ds(0, n - 1)]
        pltpu.make_async_copy(landed, landed, recv_sem.at[half]).wait()
        for a, spec in ((0, mixed_s), (1, gated_s)):
            block = jnp.concatenate([recv[holder[j], a * part:(a + 1) * part, :] for j in range(n)], axis=0)
            spec[...] = jnp.dot(block, fwd_ref[...], preferred_element_type=f32).reshape(n, part, 2 * rows)
        block = jnp.concatenate([recv[j, 2 * part:3 * part, :] for j in range(n)], axis=0)
        taps_spec = jnp.dot(block, fwd_ref[...], preferred_element_type=f32)
        before = jnp.concatenate([jnp.zeros((part, 2 * rows), f32), taps_spec[: (n - 1) * part]], axis=0)
        resp_s[...] = (before + wide_sign * taps_spec).reshape(n, part, 2 * rows)

        def tile(u, _):
            rws = pl.ds(pl.multiple_of(u * 8, 8), 8)
            zero = jnp.zeros((8, 128), f32)

            acc = [zero] * (2 * n)
            for k in range(n):
                rr, ri = resp_s[k, rws, re], resp_s[k, rws, im]
                ri0, rr2 = jnp.where(first, 0.0, ri), jnp.where(first, ri, rr)
                for p in range(k, n):
                    mr, mi = mixed_s[p - k, rws, re], mixed_s[p - k, rws, im]
                    acc[2 * p] += mr * rr - mi * ri0
                    acc[2 * p + 1] += mr * ri0 + mi * rr2
            for p in range(n):
                sum_s[p, rws, re] = acc[2 * p]
                sum_s[p, rws, im] = acc[2 * p + 1]

            acc = [zero] * (2 * n)
            for k in range(n):
                rr, ri = resp_s[k, rws, re], resp_s[k, rws, im]
                ri0, rr2 = jnp.where(first, 0.0, ri), jnp.where(first, ri, rr)
                for r in range(n - k):
                    gr, gi = gated_s[r + k, rws, re], gated_s[r + k, rws, im]
                    acc[2 * r] += gr * rr + gi * ri0
                    acc[2 * r + 1] += gi * rr2 - gr * ri0
            for r in range(n):
                sum_g[r, rws, re] = acc[2 * r]
                sum_g[r, rws, im] = acc[2 * r + 1]

            acc = [zero] * (2 * n)
            for r in range(n):
                mr, mi = mixed_s[r, rws, re], mixed_s[r, rws, im]
                mi0, mr2 = jnp.where(first, 0.0, mi), jnp.where(first, -mi, mr)
                for k in range(n - r):
                    gr, gi = gated_s[r + k, rws, re], gated_s[r + k, rws, im]
                    acc[2 * k] += mr * gr + mi0 * gi
                    acc[2 * k + 1] += mi0 * gr - mr2 * gi
            for k in range(n):
                for c, at in ((0, re), (1, im)):
                    own_sum = acc[2 * k + c]
                    if k + 1 < n:
                        own_sum = own_sum + sign * acc[2 * k + 2 + c]
                    sum_f[k, rws, at] = own_sum
            return 0

        lax.fori_loop(0, part // 8, tile, 0)

        for a, (sums, table) in enumerate(((sum_s, out_tab_ref), (sum_g, out_tab_ref), (sum_f, lag_tab_ref))):
            place = order if a < 2 else list(range(n))
            block = jnp.concatenate([sums[place[p]].astype(bf16) for p in range(n)], axis=0)
            turned = jnp.dot(block, table[...], preferred_element_type=f32)
            if a == 2:
                turned = turned * scale
            send_out[half, :, a * part:(a + 1) * part, :] = turned.astype(bf16).reshape(n, part, rows)
        for hop in hops:
            peer = peer_of(hop)
            pltpu.make_async_remote_copy(
                src_ref=send_out.at[half, peer], dst_ref=back.at[half, me],
                send_sem=back_send, recv_sem=back_recv,
                device_id={"seq": peer}, device_id_type=MESH,
            ).start()
        back[half, me] = send_out[half, me]

    landed = back.at[:, pl.ds(0, n - 1)]
    pltpu.make_async_copy(landed, landed, back_recv).wait()

    for g in range(channels // 128):
        cols = slice(g * 128, (g + 1) * 128)
        turned = []
        for a in range(3):
            pieces = []
            for i in range(128 // part):
                peer, half = (g * 128 + i * part) // own, i % HALVES
                pieces.append(back[half, peer, a * part:(a + 1) * part, :])
            turned.append(jnp.concatenate(pieces, axis=0).astype(f32).T)
        q, k, v, o = q_ref[:, cols], k_ref[:, cols], v_ref[:, cols], o_ref[:, cols]
        gain = gain_ref[:, cols]
        conv_out = turned[0] + gain * (k * v).astype(bf16).astype(f32)
        conv_grad = turned[1] + gain * (o * q).astype(bf16).astype(f32)
        hyena_ref[:, cols] = (q * conv_out).astype(bf16)
        gq_ref[:, cols] = (o * conv_out).astype(bf16)
        gk_ref[:, cols] = (conv_grad * v).astype(bf16)
        gv_ref[:, cols] = (conv_grad * k).astype(bf16)
        gf_ref[:, cols] = turned[2].astype(bf16)

    sent = send_in.at[:, pl.ds(0, n - 1)]
    pltpu.make_async_copy(sent, sent, send_sem).wait()
    sent = send_out.at[:, pl.ds(0, n - 1)]
    pltpu.make_async_copy(sent, sent, back_send).wait()


def on_device(query_proj, key_proj, value_proj, filter_taps, skip_gain, out_grad, block_order):
    n = lax.axis_size("seq")
    rows, channels = query_proj.shape
    part = channels // n // HALVES
    bf16, f32 = jnp.bfloat16, jnp.float32
    vmem = pl.BlockSpec(memory_space=pltpu.VMEM)
    tables = spectrum_tables(rows)
    spec = pltpu.VMEM((n, part, 2 * rows), f32)
    message = (HALVES, n, 3 * part, rows)
    return pl.pallas_call(
        functools.partial(kernel, n),
        out_shape=[jax.ShapeDtypeStruct((rows, channels), bf16)] * 5,
        in_specs=[vmem] * 6 + [pl.BlockSpec(memory_space=pltpu.SMEM)] + [vmem] * 3,
        out_specs=[vmem] * 5,
        scratch_shapes=[
            pltpu.VMEM(message, bf16),
            pltpu.VMEM(message[1:], bf16),
            pltpu.VMEM(message[1:], bf16),
            pltpu.VMEM(message, bf16),
            pltpu.VMEM(message, bf16),
            spec, spec, spec, spec, spec, spec,
            pltpu.SemaphoreType.DMA(()),
            pltpu.SemaphoreType.DMA((HALVES,)),
            pltpu.SemaphoreType.DMA(()),
            pltpu.SemaphoreType.DMA(()),
        ],
        compiler_params=pltpu.CompilerParams(
            collective_id=0, has_side_effects=True, vmem_limit_bytes=32 * 2**20
        ),
    )(
        query_proj, key_proj, value_proj, out_grad, filter_taps, skip_gain[None, :], block_order,
        *[jnp.asarray(t) for t in tables],
    )


def solution(mesh):
    placed = (
        P(("dp", "seq"), "chan"),
        P(("dp", "seq"), "chan"),
        P(("dp", "seq"), "chan"),
        P("seq", "chan"),
        P("chan"),
        P(("dp", "seq"), "chan"),
        P("dp"),
    )
    return jax.shard_map(
        on_device,
        mesh=mesh,
        in_specs=placed,
        out_specs=(P(("dp", "seq"), "chan"),) * 5,
        check_vma=False,
    )
```

```python
import functools
import math

import jax
import jax.numpy as jnp
import ml_dtypes
import numpy as np
from jax import lax
from jax.experimental import pallas as pl
from jax.experimental.pallas import tpu as pltpu
from jax.sharding import PartitionSpec as P

MESH = pl.DeviceIdType.MESH
HALVES = 2


def spectrum_tables(rows):
    length = 2 * rows
    time = np.arange(rows)[:, None]
    freq = np.arange(rows)[None, :]
    angle = 2.0 * np.pi / length * ((time * freq) % length)
    middle = 1.0 - 2.0 * (time % 2)
    sine = np.where(freq == 0, middle, -np.sin(angle))
    forward = np.concatenate([np.cos(angle), sine], axis=1)
    sign = 1.0 - 2.0 * (freq % 2)
    weight = np.where(freq == 0, 1.0, 2.0) / length
    output = np.concatenate([weight * sign * np.cos(angle), weight * sign * sine], axis=1).T
    lag_sine = np.where(freq == 0, middle, np.sin(angle))
    lags = np.concatenate([weight * np.cos(angle), weight * lag_sine], axis=1).T
    stacked = np.concatenate([forward[:, :rows], forward[:, rows:], output, lags], axis=0)
    return stacked.astype(ml_dtypes.bfloat16)


def exchange_kernel(
    n, q_hbm, k_hbm, v_hbm, o_hbm, taps_hbm, gain_hbm, order_hbm, tables_hbm,
    back, q_ref, k_ref, v_ref, o_ref, gain_ref,
    taps_ref, order_ref, tables, send_in, recv_a, recv_b, send_out, mixed_s, gated_s, resp_s, sum_s, sum_g, sum_f,
    load_sem, send_sem, recv_sem, back_send, back_recv,
):
    me = lax.axis_index("seq")
    rows, channels = q_ref.shape
    own = channels // n
    part = own // HALVES
    scale = 1.0 / math.sqrt(rows * n)
    bf16, f32 = jnp.bfloat16, jnp.float32

    loads = [
        pltpu.make_async_copy(src, dst, load_sem.at[i])
        for i, (src, dst) in enumerate((
            (k_hbm, k_ref), (v_hbm, v_ref), (o_hbm, o_ref), (q_hbm, q_ref), (taps_hbm, taps_ref),
            (tables_hbm, tables), (order_hbm, order_ref), (gain_hbm, gain_ref),
        ))
    ]
    for load in loads:
        load.start()

    barrier = pltpu.get_barrier_semaphore()
    for step in range(1, n):
        pl.semaphore_signal(barrier, inc=1, device_id={"seq": lax.rem(me + step, n)}, device_id_type=MESH)

    for a in range(3):
        for load in loads[2 * a : 2 * a + 2] if a < 2 else loads[4:5]:
            load.wait()
        for g in range(channels // 128):
            cols = slice(g * 128, (g + 1) * 128)
            if a == 0:
                block = k_ref[:, cols] * v_ref[:, cols]
            elif a == 1:
                block = o_ref[:, cols] * q_ref[:, cols]
            else:
                block = taps_ref[:, cols] * scale
            turned = block.T.astype(bf16)
            for i in range(128 // part):
                peer, half = (g * 128 + i * part) // own, i % HALVES
                send_in[half, peer, a * part:(a + 1) * part, :] = turned[i * part:(i + 1) * part]

    pl.semaphore_wait(barrier, n - 1)

    recvs = (recv_a, recv_b)
    hops = [(h, z) for z in (4, 3, 5, 2, 6, 1, 7, 0) for h in (1, 0) if (h, z) != (0, 0)]

    def peer_of(hop):
        h, z = hop
        ring = n // 2
        return lax.rem(me // ring + h, 2) * ring + lax.rem(me + z, ring)

    for half in range(HALVES):
        for hop in hops:
            peer = peer_of(hop)
            pltpu.make_async_remote_copy(
                src_ref=send_in.at[half, peer], dst_ref=recvs[half].at[me],
                send_sem=send_sem, recv_sem=recv_sem.at[half],
                device_id={"seq": peer}, device_id_type=MESH,
            ).start()
    for half in range(HALVES):
        recvs[half][me] = send_in[half, me]

    for load in loads[5:]:
        load.wait()
    fwd = jnp.concatenate([tables[0:rows], tables[rows : 2 * rows]], axis=1)
    out_tab, lag_tab = tables[2 * rows : 4 * rows], tables[4 * rows : 6 * rows]

    order = [order_ref[p] for p in range(n)]
    holder = []
    for j in range(n):
        at = jnp.int32(0)
        for p in range(1, n):
            at = jnp.where(order[p] == j, p, at)
        holder.append(at)

    lane = lax.broadcasted_iota(jnp.int32, (8, 128), 1)
    first = lane == 0
    sign = jnp.where(lane % 2 == 0, 1.0, -1.0).astype(f32)
    wide_lane = lax.broadcasted_iota(jnp.int32, (n * part, 2 * rows), 1)
    wide_sign = jnp.where(wide_lane % 2 == 0, 1.0, -1.0).astype(f32)
    re, im = slice(0, 128), slice(128, 256)

    for half in range(HALVES):
        recv = recvs[half]
        landed = recv.at[pl.ds(0, n - 1)]
        pltpu.make_async_copy(landed, landed, recv_sem.at[half]).wait()
        for a, spec in ((0, mixed_s), (1, gated_s)):
            block = jnp.concatenate([recv[holder[j], a * part:(a + 1) * part, :] for j in range(n)], axis=0)
            spec[...] = jnp.dot(block, fwd, preferred_element_type=f32).reshape(n, part, 2 * rows)
        block = jnp.concatenate([recv[j, 2 * part:3 * part, :] for j in range(n)], axis=0)
        taps_spec = jnp.dot(block, fwd, preferred_element_type=f32)
        before = jnp.concatenate([jnp.zeros((part, 2 * rows), f32), taps_spec[: (n - 1) * part]], axis=0)
        resp_s[...] = (before + wide_sign * taps_spec).reshape(n, part, 2 * rows)

        def tile(u, _):
            rws = pl.ds(pl.multiple_of(u * 8, 8), 8)
            zero = jnp.zeros((8, 128), f32)

            acc = [zero] * (2 * n)
            for k in range(n):
                rr, ri = resp_s[k, rws, re], resp_s[k, rws, im]
                ri0, rr2 = jnp.where(first, 0.0, ri), jnp.where(first, ri, rr)
                for p in range(k, n):
                    mr, mi = mixed_s[p - k, rws, re], mixed_s[p - k, rws, im]
                    acc[2 * p] += mr * rr - mi * ri0
                    acc[2 * p + 1] += mr * ri0 + mi * rr2
            for p in range(n):
                sum_s[p, rws, re] = acc[2 * p]
                sum_s[p, rws, im] = acc[2 * p + 1]

            acc = [zero] * (2 * n)
            for k in range(n):
                rr, ri = resp_s[k, rws, re], resp_s[k, rws, im]
                ri0, rr2 = jnp.where(first, 0.0, ri), jnp.where(first, ri, rr)
                for r in range(n - k):
                    gr, gi = gated_s[r + k, rws, re], gated_s[r + k, rws, im]
                    acc[2 * r] += gr * rr + gi * ri0
                    acc[2 * r + 1] += gi * rr2 - gr * ri0
            for r in range(n):
                sum_g[r, rws, re] = acc[2 * r]
                sum_g[r, rws, im] = acc[2 * r + 1]

            acc = [zero] * (2 * n)
            for r in range(n):
                mr, mi = mixed_s[r, rws, re], mixed_s[r, rws, im]
                mi0, mr2 = jnp.where(first, 0.0, mi), jnp.where(first, -mi, mr)
                for k in range(n - r):
                    gr, gi = gated_s[r + k, rws, re], gated_s[r + k, rws, im]
                    acc[2 * k] += mr * gr + mi0 * gi
                    acc[2 * k + 1] += mi0 * gr - mr2 * gi
            for k in range(n):
                for c, at in ((0, re), (1, im)):
                    own_sum = acc[2 * k + c]
                    if k + 1 < n:
                        own_sum = own_sum + sign * acc[2 * k + 2 + c]
                    sum_f[k, rws, at] = own_sum
            return 0

        lax.fori_loop(0, part // 8, tile, 0)

        for a, (sums, table) in enumerate(((sum_s, out_tab), (sum_g, out_tab), (sum_f, lag_tab))):
            place = order if a < 2 else list(range(n))
            block = jnp.concatenate([sums[place[p]].astype(bf16) for p in range(n)], axis=0)
            turned = jnp.dot(block, table, preferred_element_type=f32)
            if a == 2:
                turned = turned * scale
            send_out[half, :, a * part:(a + 1) * part, :] = turned.astype(bf16).reshape(n, part, rows)
        for hop in hops:
            peer = peer_of(hop)
            pltpu.make_async_remote_copy(
                src_ref=send_out.at[half, peer], dst_ref=back.at[half, me],
                send_sem=back_send, recv_sem=back_recv,
                device_id={"seq": peer}, device_id_type=MESH,
            ).start()
        back[half, me] = send_out[half, me]

    landed = back.at[:, pl.ds(0, n - 1)]
    pltpu.make_async_copy(landed, landed, back_recv).wait()

    sent = send_in.at[:, pl.ds(0, n - 1)]
    pltpu.make_async_copy(sent, sent, send_sem).wait()
    sent = send_out.at[:, pl.ds(0, n - 1)]
    pltpu.make_async_copy(sent, sent, back_send).wait()


def gate_kernel(
    n, back, q_ref, k_ref, v_ref, o_ref, gain_ref, hyena_hbm, gq_hbm, gk_hbm, gv_hbm, gf_hbm, results, sems
):
    rows, channels = q_ref.shape
    own = channels // n
    part = own // HALVES
    bf16, f32 = jnp.bfloat16, jnp.float32
    outs = (hyena_hbm, gq_hbm, gk_hbm, gv_hbm, gf_hbm)
    stores = []
    for g in range(channels // 128):
        cols = slice(g * 128, (g + 1) * 128)
        turned = []
        for a in range(3):
            pieces = []
            for i in range(128 // part):
                peer, half = (g * 128 + i * part) // own, i % HALVES
                pieces.append(back[half, peer, a * part : (a + 1) * part, :])
            turned.append(jnp.concatenate(pieces, axis=0).astype(f32).T)
        q, k, v, o = q_ref[:, cols], k_ref[:, cols], v_ref[:, cols], o_ref[:, cols]
        gain = gain_ref[:, cols]
        conv_out = turned[0] + gain * (k * v).astype(bf16).astype(f32)
        conv_grad = turned[1] + gain * (o * q).astype(bf16).astype(f32)
        values = (q * conv_out, o * conv_out, conv_grad * v, conv_grad * k, turned[2])
        for i, value in enumerate(values):
            results[i, :, cols] = value.astype(bf16)
            store = pltpu.make_async_copy(results.at[i, :, cols], outs[i].at[:, cols], sems.at[i, g])
            store.start()
            stores.append(store)
    for store in stores:
        store.wait()


def on_device(query_proj, key_proj, value_proj, filter_taps, skip_gain, out_grad, block_order):
    n = lax.axis_size("seq")
    rows, channels = query_proj.shape
    part = channels // n // HALVES
    bf16, f32 = jnp.bfloat16, jnp.float32
    vmem = pl.BlockSpec(memory_space=pltpu.VMEM)
    hbm = pl.BlockSpec(memory_space=pltpu.HBM)
    spec = pltpu.VMEM((n, part, 2 * rows), f32)
    message = (HALVES, n, 3 * part, rows)
    block = jax.ShapeDtypeStruct((rows, channels), f32)
    tables = spectrum_tables(rows)
    kept = pl.pallas_call(
        functools.partial(exchange_kernel, n),
        out_shape=[jax.ShapeDtypeStruct(message, bf16)] + [block] * 4 + [jax.ShapeDtypeStruct((1, channels), f32)],
        in_specs=[hbm] * 8,
        out_specs=[vmem] * 6,
        scratch_shapes=[
            pltpu.VMEM((rows, channels), f32),
            pltpu.SMEM((n,), jnp.int32),
            pltpu.VMEM(tables.shape, bf16),
            pltpu.VMEM(message, bf16),
            pltpu.VMEM(message[1:], bf16),
            pltpu.VMEM(message[1:], bf16),
            pltpu.VMEM(message, bf16),
            spec, spec, spec, spec, spec, spec,
            pltpu.SemaphoreType.DMA((8,)),
            pltpu.SemaphoreType.DMA(()),
            pltpu.SemaphoreType.DMA((HALVES,)),
            pltpu.SemaphoreType.DMA(()),
            pltpu.SemaphoreType.DMA(()),
        ],
        compiler_params=pltpu.CompilerParams(
            collective_id=0, has_side_effects=True, vmem_limit_bytes=32 * 2**20
        ),
        name="exchange",
    )(*[
        pltpu.with_memory_space_constraint(x, pltpu.HBM)
        for x in (
            query_proj, key_proj, value_proj, out_grad, filter_taps, skip_gain[None, :], block_order,
            jnp.asarray(tables),
        )
    ])
    result = jax.ShapeDtypeStruct((rows, channels), bf16)
    return pl.pallas_call(
        functools.partial(gate_kernel, n),
        out_shape=[result] * 5,
        in_specs=[vmem] * 6,
        out_specs=[hbm] * 5,
        scratch_shapes=[
            pltpu.VMEM((5, rows, channels), bf16),
            pltpu.SemaphoreType.DMA((5, channels // 128)),
        ],
        compiler_params=pltpu.CompilerParams(vmem_limit_bytes=32 * 2**20),
        name="gate",
    )(*kept)


def solution(mesh):
    placed = (
        P(("dp", "seq"), "chan"),
        P(("dp", "seq"), "chan"),
        P(("dp", "seq"), "chan"),
        P("seq", "chan"),
        P("chan"),
        P(("dp", "seq"), "chan"),
        P("dp"),
    )
    return jax.shard_map(
        on_device,
        mesh=mesh,
        in_specs=placed,
        out_specs=(P(("dp", "seq"), "chan"),) * 5,
        check_vma=False,
    )
```

```python
import functools
import math

import jax
import jax.numpy as jnp
import ml_dtypes
import numpy as np
from jax import lax
from jax.experimental import pallas as pl
from jax.experimental.pallas import tpu as pltpu
from jax.sharding import PartitionSpec as P

MESH = pl.DeviceIdType.MESH
HALVES = 2


def spectrum_tables(rows):
    length = 2 * rows
    time = np.arange(rows)[:, None]
    freq = np.arange(rows)[None, :]
    angle = 2.0 * np.pi / length * ((time * freq) % length)
    middle = 1.0 - 2.0 * (time % 2)
    sine = np.where(freq == 0, middle, -np.sin(angle))
    forward = np.concatenate([np.cos(angle), sine], axis=1)
    sign = 1.0 - 2.0 * (freq % 2)
    weight = np.where(freq == 0, 1.0, 2.0) / length
    output = np.concatenate([weight * sign * np.cos(angle), weight * sign * sine], axis=1).T
    lag_sine = np.where(freq == 0, middle, np.sin(angle))
    lags = np.concatenate([weight * np.cos(angle), weight * lag_sine], axis=1).T
    stacked = np.concatenate([forward[:, :rows], forward[:, rows:], output, lags], axis=0)
    return stacked.astype(ml_dtypes.bfloat16)


def exchange_kernel(
    n, q_hbm, k_hbm, v_hbm, o_hbm, taps_hbm, gain_hbm, order_hbm, tables_hbm,
    back, q_ref, k_ref, v_ref, o_ref, gain_ref,
    taps_ref, order_ref, tables, send_in, recv_tm, recv_g, recv_m2, recv_g2, recv_t2, send_out,
    mixed_s, gated_s, resp_s, sum_s, sum_f,
    load_sem, send_sem, recv_sem, pass_sem, back_send, back_recv,
):
    me, core = lax.axis_index("seq"), lax.axis_index("dp")
    rows, channels = q_ref.shape
    own = channels // n
    part = own // HALVES
    scale = 1.0 / math.sqrt(rows * n)
    bf16, f32 = jnp.bfloat16, jnp.float32

    barrier = pltpu.get_barrier_semaphore()
    for step in range(1, n):
        pl.semaphore_signal(barrier, inc=1, device_id={"seq": lax.rem(me + step, n)}, device_id_type=MESH)
    pl.semaphore_signal(barrier, inc=1, device_id={"dp": 1 - core}, device_id_type=MESH)

    loads = [
        pltpu.make_async_copy(src, dst, load_sem.at[i])
        for i, (src, dst) in enumerate((
            (taps_hbm, taps_ref), (k_hbm, k_ref), (v_hbm, v_ref), (o_hbm, o_ref), (q_hbm, q_ref),
            (tables_hbm, tables), (order_hbm, order_ref), (gain_hbm, gain_ref),
        ))
    ]
    for load in loads:
        load.start()

    def turn(a):
        for g in range(channels // 128):
            cols = slice(g * 128, (g + 1) * 128)
            if a == 0:
                block = taps_ref[:, cols] * scale
            elif a == 1:
                block = k_ref[:, cols] * v_ref[:, cols]
            else:
                block = o_ref[:, cols] * q_ref[:, cols]
            turned = block.T.astype(bf16)
            for i in range(128 // part):
                peer, half = (g * 128 + i * part) // own, i % HALVES
                send_in[half, peer, a * part : (a + 1) * part, :] = turned[i * part : (i + 1) * part]

    hops = [(h, z) for z in (4, 3, 5, 2, 6, 1, 7, 0) for h in (1, 0) if (h, z) != (0, 0)]

    def send_all(source, target, send, recv):
        ring = n // 2
        for h, z in hops:
            peer = lax.rem(me // ring + h, 2) * ring + lax.rem(me + z, ring)
            pltpu.make_async_remote_copy(
                src_ref=source(peer), dst_ref=target, send_sem=send, recv_sem=recv,
                device_id={"seq": peer}, device_id_type=MESH,
            ).start()

    early, late = core, 1 - core
    inputs = (
        (early, 0, 2 * part, recv_tm), (early, 2 * part, part, recv_g),
        (late, part, part, recv_m2), (late, 2 * part, part, recv_g2),
    )

    def send_input(i):
        half, start, size, recv = inputs[i]
        rws = pl.ds(start, size)
        send_all(lambda peer: send_in.at[half, peer, rws], recv.at[me], send_sem, recv_sem.at[i])
        recv[me] = send_in[half, me, rws, :]

    def wait_input(i):
        landed = inputs[i][3].at[pl.ds(0, n - 1)]
        pltpu.make_async_copy(landed, landed, recv_sem.at[i]).wait()

    loads[0].wait()
    turn(0)
    loads[1].wait()
    loads[2].wait()
    turn(1)
    pl.semaphore_wait(barrier, n)
    send_input(0)
    loads[3].wait()
    loads[4].wait()
    turn(2)
    for i in range(1, 4):
        send_input(i)

    for load in loads[5:]:
        load.wait()
    fwd = jnp.concatenate([tables[0:rows], tables[rows : 2 * rows]], axis=1)
    out_tab, lag_tab = tables[2 * rows : 4 * rows], tables[4 * rows : 6 * rows]

    order = [order_ref[p] for p in range(n)]
    holder = []
    for j in range(n):
        at = jnp.int32(0)
        for p in range(1, n):
            at = jnp.where(order[p] == j, p, at)
        holder.append(at)
    plain = list(range(n))

    lane = lax.broadcasted_iota(jnp.int32, (8, 128), 1)
    first = lane == 0
    sign = jnp.where(lane % 2 == 0, 1.0, -1.0).astype(f32)
    wide_lane = lax.broadcasted_iota(jnp.int32, (n * part, 2 * rows), 1)
    wide_sign = jnp.where(wide_lane % 2 == 0, 1.0, -1.0).astype(f32)
    re, im = slice(0, 128), slice(128, 256)
    zero = jnp.zeros((8, 128), f32)

    def spectra(recv, start, places):
        block = jnp.concatenate([recv[places[j], start : start + part, :] for j in range(n)], axis=0)
        return jnp.dot(block, fwd, preferred_element_type=f32)

    def response(recv):
        taps_spec = spectra(recv, 0, plain)
        before = jnp.concatenate([jnp.zeros((part, 2 * rows), f32), taps_spec[: (n - 1) * part]], axis=0)
        resp_s[...] = (before + wide_sign * taps_spec).reshape(n, part, 2 * rows)

    def tiles(body):
        def step(u, _):
            body(pl.ds(pl.multiple_of(u * 8, 8), 8))
            return 0

        lax.fori_loop(0, part // 8, step, 0)

    def forward_tile(rws):
        acc = [zero] * (2 * n)
        for k in range(n):
            rr, ri = resp_s[k, rws, re], resp_s[k, rws, im]
            ri0, rr2 = jnp.where(first, 0.0, ri), jnp.where(first, ri, rr)
            for p in range(k, n):
                mr, mi = mixed_s[p - k, rws, re], mixed_s[p - k, rws, im]
                acc[2 * p] += mr * rr - mi * ri0
                acc[2 * p + 1] += mr * ri0 + mi * rr2
        for p in range(n):
            sum_s[p, rws, re] = acc[2 * p]
            sum_s[p, rws, im] = acc[2 * p + 1]

    def backward_tile(rws):
        acc = [zero] * (2 * n)
        for k in range(n):
            rr, ri = resp_s[k, rws, re], resp_s[k, rws, im]
            ri0, rr2 = jnp.where(first, 0.0, ri), jnp.where(first, ri, rr)
            for r in range(n - k):
                gr, gi = gated_s[r + k, rws, re], gated_s[r + k, rws, im]
                acc[2 * r] += gr * rr + gi * ri0
                acc[2 * r + 1] += gi * rr2 - gr * ri0
        for r in range(n):
            sum_s[r, rws, re] = acc[2 * r]
            sum_s[r, rws, im] = acc[2 * r + 1]

        acc = [zero] * (2 * n)
        for r in range(n):
            mr, mi = mixed_s[r, rws, re], mixed_s[r, rws, im]
            mi0, mr2 = jnp.where(first, 0.0, mi), jnp.where(first, -mi, mr)
            for k in range(n - r):
                gr, gi = gated_s[r + k, rws, re], gated_s[r + k, rws, im]
                acc[2 * k] += mr * gr + mi0 * gi
                acc[2 * k + 1] += mi0 * gr - mr2 * gi
        for k in range(n):
            for c, at in ((0, re), (1, im)):
                own_sum = acc[2 * k + c]
                if k + 1 < n:
                    own_sum = own_sum + sign * acc[2 * k + 2 + c]
                sum_f[k, rws, at] = own_sum

    def result(half, a, sums, table, places, factor=None):
        block = jnp.concatenate([sums[places[p]].astype(bf16) for p in range(n)], axis=0)
        values = jnp.dot(block, table, preferred_element_type=f32)
        if factor is not None:
            values = values * factor
        send_out[half, :, a * part : (a + 1) * part, :] = values.astype(bf16).reshape(n, part, rows)

    def send_result(half, start, size):
        rws = pl.ds(start, size)
        send_all(lambda peer: send_out.at[half, peer, rws], back.at[half, me, rws], back_send, back_recv)
        back[half, me, rws, :] = send_out[half, me, rws, :]

    def convolve(half, mixed_in, mixed_start, taps_in):
        response(taps_in)
        mixed_s[...] = spectra(mixed_in, mixed_start, holder).reshape(n, part, 2 * rows)
        tiles(forward_tile)
        result(half, 0, sum_s, out_tab, order)
        send_result(half, 0, part)

    def correlate(half, gated_in):
        gated_s[...] = spectra(gated_in, 0, holder).reshape(n, part, 2 * rows)
        tiles(backward_tile)
        result(half, 1, sum_s, out_tab, order)
        result(half, 2, sum_f, lag_tab, plain, scale)
        send_result(half, part, 2 * part)

    wait_input(0)
    pass_on = pltpu.make_async_remote_copy(
        src_ref=recv_tm.at[:, pl.ds(0, part)], dst_ref=recv_t2,
        send_sem=pass_sem.at[0], recv_sem=pass_sem.at[1],
        device_id={"dp": 1 - core}, device_id_type=MESH,
    )
    pass_on.start()
    convolve(early, recv_tm, part, recv_tm)
    wait_input(1)
    correlate(early, recv_g)
    pass_on.wait()
    wait_input(2)
    convolve(late, recv_m2, 0, recv_t2)
    wait_input(3)
    correlate(late, recv_g2)

    landed = back.at[:, pl.ds(0, n - 1)]
    pltpu.make_async_copy(landed, landed, back_recv).wait()
    for _, _, _, recv in inputs:
        sent = recv.at[pl.ds(0, n - 1)]
        pltpu.make_async_copy(sent, sent, send_sem).wait()
    sent = send_out.at[:, pl.ds(0, n - 1)]
    pltpu.make_async_copy(sent, sent, back_send).wait()


def gate_kernel(
    n, back, q_ref, k_ref, v_ref, o_ref, gain_ref, hyena_hbm, gq_hbm, gk_hbm, gv_hbm, gf_hbm, results, sems
):
    rows, channels = q_ref.shape
    own = channels // n
    part = own // HALVES
    bf16, f32 = jnp.bfloat16, jnp.float32
    outs = (hyena_hbm, gq_hbm, gk_hbm, gv_hbm, gf_hbm)
    stores = []
    for g in range(channels // 128):
        cols = slice(g * 128, (g + 1) * 128)
        turned = []
        for a in range(3):
            pieces = []
            for i in range(128 // part):
                peer, half = (g * 128 + i * part) // own, i % HALVES
                pieces.append(back[half, peer, a * part : (a + 1) * part, :])
            turned.append(jnp.concatenate(pieces, axis=0).astype(f32).T)
        q, k, v, o = q_ref[:, cols], k_ref[:, cols], v_ref[:, cols], o_ref[:, cols]
        gain = gain_ref[:, cols]
        conv_out = turned[0] + gain * (k * v).astype(bf16).astype(f32)
        conv_grad = turned[1] + gain * (o * q).astype(bf16).astype(f32)
        values = (q * conv_out, o * conv_out, conv_grad * v, conv_grad * k, turned[2])
        for i, value in enumerate(values):
            results[i, :, cols] = value.astype(bf16)
            store = pltpu.make_async_copy(results.at[i, :, cols], outs[i].at[:, cols], sems.at[i, g])
            store.start()
            stores.append(store)
    for store in stores:
        store.wait()


def on_device(query_proj, key_proj, value_proj, filter_taps, skip_gain, out_grad, block_order):
    n = lax.axis_size("seq")
    rows, channels = query_proj.shape
    part = channels // n // HALVES
    bf16, f32 = jnp.bfloat16, jnp.float32
    vmem = pl.BlockSpec(memory_space=pltpu.VMEM)
    hbm = pl.BlockSpec(memory_space=pltpu.HBM)
    spec = pltpu.VMEM((n, part, 2 * rows), f32)
    small = pltpu.VMEM((n, part, rows), bf16)
    message = (HALVES, n, 3 * part, rows)
    block = jax.ShapeDtypeStruct((rows, channels), f32)
    tables = spectrum_tables(rows)
    kept = pl.pallas_call(
        functools.partial(exchange_kernel, n),
        out_shape=[jax.ShapeDtypeStruct(message, bf16)] + [block] * 4 + [jax.ShapeDtypeStruct((1, channels), f32)],
        in_specs=[hbm] * 8,
        out_specs=[vmem] * 6,
        scratch_shapes=[
            pltpu.VMEM((rows, channels), f32),
            pltpu.SMEM((n,), jnp.int32),
            pltpu.VMEM(tables.shape, bf16),
            pltpu.VMEM(message, bf16),
            pltpu.VMEM((n, 2 * part, rows), bf16),
            small, small, small, small,
            pltpu.VMEM(message, bf16),
            spec, spec, spec, spec, spec,
            pltpu.SemaphoreType.DMA((8,)),
            pltpu.SemaphoreType.DMA(()),
            pltpu.SemaphoreType.DMA((4,)),
            pltpu.SemaphoreType.DMA((2,)),
            pltpu.SemaphoreType.DMA(()),
            pltpu.SemaphoreType.DMA(()),
        ],
        compiler_params=pltpu.CompilerParams(
            collective_id=0, has_side_effects=True, vmem_limit_bytes=32 * 2**20
        ),
        name="exchange",
    )(*[
        pltpu.with_memory_space_constraint(x, pltpu.HBM)
        for x in (
            query_proj, key_proj, value_proj, out_grad, filter_taps, skip_gain[None, :], block_order,
            jnp.asarray(tables),
        )
    ])
    result = jax.ShapeDtypeStruct((rows, channels), bf16)
    return pl.pallas_call(
        functools.partial(gate_kernel, n),
        out_shape=[result] * 5,
        in_specs=[vmem] * 6,
        out_specs=[hbm] * 5,
        scratch_shapes=[
            pltpu.VMEM((5, rows, channels), bf16),
            pltpu.SemaphoreType.DMA((5, channels // 128)),
        ],
        compiler_params=pltpu.CompilerParams(vmem_limit_bytes=32 * 2**20),
        name="gate",
    )(*kept)


def solution(mesh):
    placed = (
        P(("dp", "seq"), "chan"),
        P(("dp", "seq"), "chan"),
        P(("dp", "seq"), "chan"),
        P("seq", "chan"),
        P("chan"),
        P(("dp", "seq"), "chan"),
        P("dp"),
    )
    return jax.shard_map(
        on_device,
        mesh=mesh,
        in_specs=placed,
        out_specs=(P(("dp", "seq"), "chan"),) * 5,
        check_vma=False,
    )
```

```python
import functools
import math

import jax
import jax.numpy as jnp
import ml_dtypes
import numpy as np
from jax import lax
from jax.experimental import pallas as pl
from jax.experimental.pallas import tpu as pltpu
from jax.sharding import PartitionSpec as P

MESH = pl.DeviceIdType.MESH
HALVES = 2


def spectrum_tables(rows):
    length = 2 * rows
    time = np.arange(rows)[:, None]
    freq = np.arange(rows)[None, :]
    angle = 2.0 * np.pi / length * ((time * freq) % length)
    middle = 1.0 - 2.0 * (time % 2)
    sine = np.where(freq == 0, middle, -np.sin(angle))
    forward = np.concatenate([np.cos(angle), sine], axis=1)
    sign = 1.0 - 2.0 * (freq % 2)
    weight = np.where(freq == 0, 1.0, 2.0) / length
    output = np.concatenate([weight * sign * np.cos(angle), weight * sign * sine], axis=1).T
    lag_sine = np.where(freq == 0, middle, np.sin(angle))
    lags = np.concatenate([weight * np.cos(angle), weight * lag_sine], axis=1).T
    stacked = np.concatenate([forward[:, :rows], forward[:, rows:], output, lags], axis=0)
    return stacked.astype(ml_dtypes.bfloat16)


def exchange_kernel(
    n, q_hbm, k_hbm, v_hbm, o_hbm, taps_hbm, gain_hbm, order_hbm, tables_hbm,
    back, q_ref, k_ref, v_ref, o_ref, gain_ref,
    taps_ref, order_ref, tables, send_in, recv_tm, recv_g, recv_m2, recv_g2, recv_t2, send_out,
    mixed_s, gated_s, resp_s, sum_s, sum_f,
    load_sem, send_sem, recv_sem, pass_sem, back_send, back_recv,
):
    me, core = lax.axis_index("seq"), lax.axis_index("dp")
    rows, channels = q_ref.shape
    own = channels // n
    part = own // HALVES
    scale = 1.0 / math.sqrt(rows * n)
    bf16, f32 = jnp.bfloat16, jnp.float32

    barrier = pltpu.get_barrier_semaphore()
    for step in range(1, n):
        pl.semaphore_signal(barrier, inc=1, device_id={"seq": lax.rem(me + step, n)}, device_id_type=MESH)
    pl.semaphore_signal(barrier, inc=1, device_id={"dp": 1 - core}, device_id_type=MESH)

    loads = [
        pltpu.make_async_copy(src, dst, load_sem.at[i])
        for i, (src, dst) in enumerate((
            (taps_hbm, taps_ref), (k_hbm, k_ref), (v_hbm, v_ref), (o_hbm, o_ref), (q_hbm, q_ref),
            (tables_hbm, tables), (order_hbm, order_ref), (gain_hbm, gain_ref),
        ))
    ]
    for load in loads:
        load.start()

    def turn(a):
        for g in range(channels // 128):
            cols = slice(g * 128, (g + 1) * 128)
            if a == 0:
                block = taps_ref[:, cols] * scale
            elif a == 1:
                block = k_ref[:, cols] * v_ref[:, cols]
            else:
                block = o_ref[:, cols] * q_ref[:, cols]
            turned = block.T.astype(bf16)
            for i in range(128 // part):
                peer, half = (g * 128 + i * part) // own, i % HALVES
                send_in[half, peer, a * part : (a + 1) * part, :] = turned[i * part : (i + 1) * part]

    hops = [(h, z) for h in (1, 0) for z in (4, 3, 5, 2, 6, 1, 7, 0) if (h, z) != (0, 0)]

    ring = n // 2
    peers = {
        (h, z): lax.rem(me // ring + h, 2) * ring + lax.rem(me + z, ring) for h, z in hops
    }

    def send_all(source, target, send, recv, group=None):
        for hop in group or hops:
            peer = peers[hop]
            pltpu.make_async_remote_copy(
                src_ref=source(peer), dst_ref=target, send_sem=send, recv_sem=recv,
                device_id={"seq": peer}, device_id_type=MESH,
            ).start()

    early, late = core, 1 - core
    inputs = (
        (early, 0, 2 * part, recv_tm), (early, 2 * part, part, recv_g),
        (late, part, 2 * part, recv_m2),
    )

    far = [(h, z) for h, z in hops if 2 * h + min(z, 8 - z) >= 5]
    near = [hop for hop in hops if hop not in far]

    def send_input(i, group=None):
        half, start, size, recv = inputs[i]
        rws = pl.ds(start, size)
        send_all(lambda peer: send_in.at[half, peer, rws], recv.at[me], send_sem, recv_sem.at[i], group)
        if group is not near:
            recv[me] = send_in[half, me, rws, :]

    def wait_input(i):
        landed = inputs[i][3].at[pl.ds(0, n - 1)]
        pltpu.make_async_copy(landed, landed, recv_sem.at[i]).wait()

    loads[0].wait()
    turn(0)
    loads[1].wait()
    loads[2].wait()
    turn(1)
    loads[3].wait()
    loads[4].wait()
    turn(2)
    pl.semaphore_wait(barrier, n)
    for group in (far, near):
        send_input(0, group)
        send_input(1, group)
    send_input(2)

    for load in loads[5:]:
        load.wait()
    fwd = jnp.concatenate([tables[0:rows], tables[rows : 2 * rows]], axis=1)
    out_tab, lag_tab = tables[2 * rows : 4 * rows], tables[4 * rows : 6 * rows]

    order = [order_ref[p] for p in range(n)]
    holder = []
    for j in range(n):
        at = jnp.int32(0)
        for p in range(1, n):
            at = jnp.where(order[p] == j, p, at)
        holder.append(at)
    plain = list(range(n))

    lane = lax.broadcasted_iota(jnp.int32, (8, 128), 1)
    first = lane == 0
    sign = jnp.where(lane % 2 == 0, 1.0, -1.0).astype(f32)
    wide_lane = lax.broadcasted_iota(jnp.int32, (n * part, 2 * rows), 1)
    wide_sign = jnp.where(wide_lane % 2 == 0, 1.0, -1.0).astype(f32)
    re, im = slice(0, 128), slice(128, 256)
    zero = jnp.zeros((8, 128), f32)

    def spectra(recv, start, places):
        block = jnp.concatenate([recv[places[j], start : start + part, :] for j in range(n)], axis=0)
        return jnp.dot(block, fwd, preferred_element_type=f32)

    def response(recv):
        taps_spec = spectra(recv, 0, plain)
        before = jnp.concatenate([jnp.zeros((part, 2 * rows), f32), taps_spec[: (n - 1) * part]], axis=0)
        resp_s[...] = (before + wide_sign * taps_spec).reshape(n, part, 2 * rows)

    def tiles(body):
        def step(u, _):
            body(pl.ds(pl.multiple_of(u * 8, 8), 8))
            return 0

        lax.fori_loop(0, part // 8, step, 0)

    def forward_tile(rws):
        acc = [zero] * (2 * n)
        for k in range(n):
            rr, ri = resp_s[k, rws, re], resp_s[k, rws, im]
            ri0, rr2 = jnp.where(first, 0.0, ri), jnp.where(first, ri, rr)
            for p in range(k, n):
                mr, mi = mixed_s[p - k, rws, re], mixed_s[p - k, rws, im]
                acc[2 * p] += mr * rr - mi * ri0
                acc[2 * p + 1] += mr * ri0 + mi * rr2
        for p in range(n):
            sum_s[p, rws, re] = acc[2 * p]
            sum_s[p, rws, im] = acc[2 * p + 1]

    def backward_tile(rws):
        acc = [zero] * (2 * n)
        for k in range(n):
            rr, ri = resp_s[k, rws, re], resp_s[k, rws, im]
            ri0, rr2 = jnp.where(first, 0.0, ri), jnp.where(first, ri, rr)
            for r in range(n - k):
                gr, gi = gated_s[r + k, rws, re], gated_s[r + k, rws, im]
                acc[2 * r] += gr * rr + gi * ri0
                acc[2 * r + 1] += gi * rr2 - gr * ri0
        for r in range(n):
            sum_s[r, rws, re] = acc[2 * r]
            sum_s[r, rws, im] = acc[2 * r + 1]

        acc = [zero] * (2 * n)
        for r in range(n):
            mr, mi = mixed_s[r, rws, re], mixed_s[r, rws, im]
            mi0, mr2 = jnp.where(first, 0.0, mi), jnp.where(first, -mi, mr)
            for k in range(n - r):
                gr, gi = gated_s[r + k, rws, re], gated_s[r + k, rws, im]
                acc[2 * k] += mr * gr + mi0 * gi
                acc[2 * k + 1] += mi0 * gr - mr2 * gi
        for k in range(n):
            for c, at in ((0, re), (1, im)):
                own_sum = acc[2 * k + c]
                if k + 1 < n:
                    own_sum = own_sum + sign * acc[2 * k + 2 + c]
                sum_f[k, rws, at] = own_sum

    def result(half, a, sums, table, places, factor=None):
        block = jnp.concatenate([sums[places[p]].astype(bf16) for p in range(n)], axis=0)
        values = jnp.dot(block, table, preferred_element_type=f32)
        if factor is not None:
            values = values * factor
        send_out[half, :, a * part : (a + 1) * part, :] = values.astype(bf16).reshape(n, part, rows)

    def send_result(half, start, size):
        rws = pl.ds(start, size)
        send_all(lambda peer: send_out.at[half, peer, rws], back.at[half, me, rws], back_send, back_recv)
        back[half, me, rws, :] = send_out[half, me, rws, :]

    def convolve(half, mixed_in, mixed_start, taps_in):
        response(taps_in)
        mixed_s[...] = spectra(mixed_in, mixed_start, holder).reshape(n, part, 2 * rows)
        tiles(forward_tile)
        result(half, 0, sum_s, out_tab, order)
        send_result(half, 0, part)

    def correlate(half, gated_in, start=0):
        gated_s[...] = spectra(gated_in, start, holder).reshape(n, part, 2 * rows)
        tiles(backward_tile)
        result(half, 1, sum_s, out_tab, order)
        result(half, 2, sum_f, lag_tab, plain, scale)
        send_result(half, part, 2 * part)

    wait_input(0)
    pass_on = pltpu.make_async_remote_copy(
        src_ref=recv_tm.at[:, pl.ds(0, part)], dst_ref=recv_t2,
        send_sem=pass_sem.at[0], recv_sem=pass_sem.at[1],
        device_id={"dp": 1 - core}, device_id_type=MESH,
    )
    pass_on.start()
    convolve(early, recv_tm, part, recv_tm)
    wait_input(1)
    correlate(early, recv_g)
    pass_on.wait()
    wait_input(2)
    convolve(late, recv_m2, 0, recv_t2)
    correlate(late, recv_m2, part)

    landed = back.at[:, pl.ds(0, n - 1)]
    pltpu.make_async_copy(landed, landed, back_recv).wait()
    for _, _, _, recv in inputs:
        sent = recv.at[pl.ds(0, n - 1)]
        pltpu.make_async_copy(sent, sent, send_sem).wait()
    sent = send_out.at[:, pl.ds(0, n - 1)]
    pltpu.make_async_copy(sent, sent, back_send).wait()


def gate_kernel(
    n, back, q_ref, k_ref, v_ref, o_ref, gain_ref, hyena_hbm, gq_hbm, gk_hbm, gv_hbm, gf_hbm, results, sems
):
    rows, channels = q_ref.shape
    own = channels // n
    part = own // HALVES
    bf16, f32 = jnp.bfloat16, jnp.float32
    outs = (hyena_hbm, gq_hbm, gk_hbm, gv_hbm, gf_hbm)
    stores = []
    for g in range(channels // 128):
        cols = slice(g * 128, (g + 1) * 128)
        turned = []
        for a in range(3):
            pieces = []
            for i in range(128 // part):
                peer, half = (g * 128 + i * part) // own, i % HALVES
                pieces.append(back[half, peer, a * part : (a + 1) * part, :])
            turned.append(jnp.concatenate(pieces, axis=0).astype(f32).T)
        q, k, v, o = q_ref[:, cols], k_ref[:, cols], v_ref[:, cols], o_ref[:, cols]
        gain = gain_ref[:, cols]
        conv_out = turned[0] + gain * (k * v).astype(bf16).astype(f32)
        conv_grad = turned[1] + gain * (o * q).astype(bf16).astype(f32)
        values = (q * conv_out, o * conv_out, conv_grad * v, conv_grad * k, turned[2])
        for i, value in enumerate(values):
            results[i, :, cols] = value.astype(bf16)
            store = pltpu.make_async_copy(results.at[i, :, cols], outs[i].at[:, cols], sems.at[i, g])
            store.start()
            stores.append(store)
    for store in stores:
        store.wait()


def on_device(query_proj, key_proj, value_proj, filter_taps, skip_gain, out_grad, block_order):
    n = lax.axis_size("seq")
    rows, channels = query_proj.shape
    part = channels // n // HALVES
    bf16, f32 = jnp.bfloat16, jnp.float32
    vmem = pl.BlockSpec(memory_space=pltpu.VMEM)
    hbm = pl.BlockSpec(memory_space=pltpu.HBM)
    spec = pltpu.VMEM((n, part, 2 * rows), f32)
    small = pltpu.VMEM((n, part, rows), bf16)
    message = (HALVES, n, 3 * part, rows)
    block = jax.ShapeDtypeStruct((rows, channels), f32)
    tables = spectrum_tables(rows)
    kept = pl.pallas_call(
        functools.partial(exchange_kernel, n),
        out_shape=[jax.ShapeDtypeStruct(message, bf16)] + [block] * 4 + [jax.ShapeDtypeStruct((1, channels), f32)],
        in_specs=[hbm] * 8,
        out_specs=[vmem] * 6,
        scratch_shapes=[
            pltpu.VMEM((rows, channels), f32),
            pltpu.SMEM((n,), jnp.int32),
            pltpu.VMEM(tables.shape, bf16),
            pltpu.VMEM(message, bf16),
            pltpu.VMEM((n, 2 * part, rows), bf16),
            small, pltpu.VMEM((n, 2 * part, rows), bf16), small, small,
            pltpu.VMEM(message, bf16),
            spec, spec, spec, spec, spec,
            pltpu.SemaphoreType.DMA((8,)),
            pltpu.SemaphoreType.DMA(()),
            pltpu.SemaphoreType.DMA((4,)),
            pltpu.SemaphoreType.DMA((2,)),
            pltpu.SemaphoreType.DMA(()),
            pltpu.SemaphoreType.DMA(()),
        ],
        compiler_params=pltpu.CompilerParams(
            collective_id=0, has_side_effects=True, vmem_limit_bytes=32 * 2**20
        ),
        name="exchange",
    )(*[
        pltpu.with_memory_space_constraint(x, pltpu.HBM)
        for x in (
            query_proj, key_proj, value_proj, out_grad, filter_taps, skip_gain[None, :], block_order,
            jnp.asarray(tables),
        )
    ])
    result = jax.ShapeDtypeStruct((rows, channels), bf16)
    return pl.pallas_call(
        functools.partial(gate_kernel, n),
        out_shape=[result] * 5,
        in_specs=[vmem] * 6,
        out_specs=[hbm] * 5,
        scratch_shapes=[
            pltpu.VMEM((5, rows, channels), bf16),
            pltpu.SemaphoreType.DMA((5, channels // 128)),
        ],
        compiler_params=pltpu.CompilerParams(vmem_limit_bytes=32 * 2**20),
        name="gate",
    )(*kept)


def solution(mesh):
    placed = (
        P(("dp", "seq"), "chan"),
        P(("dp", "seq"), "chan"),
        P(("dp", "seq"), "chan"),
        P("seq", "chan"),
        P("chan"),
        P(("dp", "seq"), "chan"),
        P("dp"),
    )
    return jax.shard_map(
        on_device,
        mesh=mesh,
        in_specs=placed,
        out_specs=(P(("dp", "seq"), "chan"),) * 5,
        check_vma=False,
    )
```

```python
import functools
import math

import jax
import jax.numpy as jnp
import ml_dtypes
import numpy as np
from jax import lax
from jax.experimental import pallas as pl
from jax.experimental.pallas import tpu as pltpu
from jax.sharding import PartitionSpec as P

MESH = pl.DeviceIdType.MESH
HALVES = 2


def spectrum_tables(rows):
    length = 2 * rows
    time = np.arange(rows)[:, None]
    freq = np.arange(rows)[None, :]
    angle = 2.0 * np.pi / length * ((time * freq) % length)
    middle = 1.0 - 2.0 * (time % 2)
    sine = np.where(freq == 0, middle, -np.sin(angle))
    forward = np.concatenate([np.cos(angle), sine], axis=1)
    sign = 1.0 - 2.0 * (freq % 2)
    weight = np.where(freq == 0, 1.0, 2.0) / length
    output = np.concatenate([weight * sign * np.cos(angle), weight * sign * sine], axis=1).T
    lag_sine = np.where(freq == 0, middle, np.sin(angle))
    lags = np.concatenate([weight * np.cos(angle), weight * lag_sine], axis=1).T
    stacked = np.concatenate([forward[:, :rows], forward[:, rows:], output, lags], axis=0)
    return stacked.astype(ml_dtypes.bfloat16)


def gated_group(back, half, g, q_ref, k_ref, v_ref, o_ref, gain_ref):
    part = back.shape[2] // 3
    wide = q_ref.shape[1] // HALVES
    bf16, f32 = jnp.bfloat16, jnp.float32
    turned = []
    for a in range(3):
        pieces = [back[half, g * (128 // part) + i, a * part : (a + 1) * part, :] for i in range(128 // part)]
        turned.append(jnp.concatenate(pieces, axis=0).astype(f32).T)
    lanes = pl.ds(pl.multiple_of(half * wide + g * 128, 128), 128)
    q, k, v, o = q_ref[:, lanes], k_ref[:, lanes], v_ref[:, lanes], o_ref[:, lanes]
    gain = gain_ref[:, lanes]
    conv_out = turned[0] + gain * (k * v).astype(bf16).astype(f32)
    conv_grad = turned[1] + gain * (o * q).astype(bf16).astype(f32)
    values = (q * conv_out, o * conv_out, conv_grad * v, conv_grad * k, turned[2])
    return [value.astype(bf16) for value in values]


def exchange_kernel(
    n, q_hbm, k_hbm, v_hbm, o_hbm, taps_hbm, gain_hbm, order_hbm, tables_hbm,
    back, first_half, q_ref, k_ref, v_ref, o_ref, gain_ref,
    taps_ref, order_ref, tables, send_in, recv_tm, recv_g, recv_m2, recv_g2, recv_t2, send_out,
    mixed_s, gated_s, resp_s, sum_s, sum_f,
    load_sem, send_sem, recv_sem, pass_sem, back_send, back_recv,
):
    me, core = lax.axis_index("seq"), lax.axis_index("dp")
    rows, channels = q_ref.shape
    own = channels // n
    part = own // HALVES
    wide = channels // HALVES
    scale = 1.0 / math.sqrt(rows * n)
    bf16, f32 = jnp.bfloat16, jnp.float32

    barrier = pltpu.get_barrier_semaphore()
    for step in range(1, n):
        pl.semaphore_signal(barrier, inc=1, device_id={"seq": lax.rem(me + step, n)}, device_id_type=MESH)
    pl.semaphore_signal(barrier, inc=1, device_id={"dp": 1 - core}, device_id_type=MESH)

    loads = [
        pltpu.make_async_copy(src, dst, load_sem.at[i])
        for i, (src, dst) in enumerate((
            (taps_hbm, taps_ref), (k_hbm, k_ref), (v_hbm, v_ref), (o_hbm, o_ref), (q_hbm, q_ref),
            (tables_hbm, tables), (order_hbm, order_ref), (gain_hbm, gain_ref),
        ))
    ]
    for load in loads:
        load.start()

    def turn(a):
        for g in range(channels // 128):
            cols = slice(g * 128, (g + 1) * 128)
            if a == 0:
                block = taps_ref[:, cols] * scale
            elif a == 1:
                block = k_ref[:, cols] * v_ref[:, cols]
            else:
                block = o_ref[:, cols] * q_ref[:, cols]
            turned = block.T.astype(bf16)
            for i in range(128 // part):
                half, peer = divmod(g * (128 // part) + i, n)
                send_in[half, peer, a * part : (a + 1) * part, :] = turned[i * part : (i + 1) * part]

    hops = [(h, z) for h in (1, 0) for z in (4, 3, 5, 2, 6, 1, 7, 0) if (h, z) != (0, 0)]

    ring = n // 2
    peers = {
        (h, z): lax.rem(me // ring + h, 2) * ring + lax.rem(me + z, ring) for h, z in hops
    }

    def send_all(source, target, send, recv, group=None):
        for hop in group or hops:
            peer = peers[hop]
            pltpu.make_async_remote_copy(
                src_ref=source(peer), dst_ref=target, send_sem=send, recv_sem=recv,
                device_id={"seq": peer}, device_id_type=MESH,
            ).start()

    early, late = core, 1 - core
    inputs = (
        (early, 0, 2 * part, recv_tm), (early, 2 * part, part, recv_g),
        (late, part, 2 * part, recv_m2),
    )

    far = [(h, z) for h, z in hops if 2 * h + min(z, 8 - z) >= 5]
    near = [hop for hop in hops if hop not in far]

    def send_input(i, group=None):
        half, start, size, recv = inputs[i]
        rws = pl.ds(start, size)
        send_all(lambda peer: send_in.at[half, peer, rws], recv.at[me], send_sem, recv_sem.at[i], group)
        if group is not near:
            recv[me] = send_in[half, me, rws, :]

    def wait_input(i):
        landed = inputs[i][3].at[pl.ds(0, n - 1)]
        pltpu.make_async_copy(landed, landed, recv_sem.at[i]).wait()

    loads[0].wait()
    turn(0)
    loads[1].wait()
    loads[2].wait()
    turn(1)
    loads[3].wait()
    loads[4].wait()
    turn(2)
    pl.semaphore_wait(barrier, n)
    for group in (far, near):
        send_input(0, group)
        send_input(1, group)
    send_input(2)

    for load in loads[5:]:
        load.wait()
    fwd = jnp.concatenate([tables[0:rows], tables[rows : 2 * rows]], axis=1)
    out_tab, lag_tab = tables[2 * rows : 4 * rows], tables[4 * rows : 6 * rows]

    order = [order_ref[p] for p in range(n)]
    holder = []
    for j in range(n):
        at = jnp.int32(0)
        for p in range(1, n):
            at = jnp.where(order[p] == j, p, at)
        holder.append(at)
    plain = list(range(n))

    lane = lax.broadcasted_iota(jnp.int32, (8, 128), 1)
    first = lane == 0
    sign = jnp.where(lane % 2 == 0, 1.0, -1.0).astype(f32)
    wide_lane = lax.broadcasted_iota(jnp.int32, (n * part, 2 * rows), 1)
    wide_sign = jnp.where(wide_lane % 2 == 0, 1.0, -1.0).astype(f32)
    re, im = slice(0, 128), slice(128, 256)
    zero = jnp.zeros((8, 128), f32)

    def spectra(recv, start, places):
        block = jnp.concatenate([recv[places[j], start : start + part, :] for j in range(n)], axis=0)
        return jnp.dot(block, fwd, preferred_element_type=f32)

    def response(recv):
        taps_spec = spectra(recv, 0, plain)
        before = jnp.concatenate([jnp.zeros((part, 2 * rows), f32), taps_spec[: (n - 1) * part]], axis=0)
        resp_s[...] = (before + wide_sign * taps_spec).reshape(n, part, 2 * rows)

    def tiles(body):
        def step(u, _):
            body(pl.ds(pl.multiple_of(u * 8, 8), 8))
            return 0

        lax.fori_loop(0, part // 8, step, 0)

    def forward_tile(rws):
        acc = [zero] * (2 * n)
        for k in range(n):
            rr, ri = resp_s[k, rws, re], resp_s[k, rws, im]
            ri0, rr2 = jnp.where(first, 0.0, ri), jnp.where(first, ri, rr)
            for p in range(k, n):
                mr, mi = mixed_s[p - k, rws, re], mixed_s[p - k, rws, im]
                acc[2 * p] += mr * rr - mi * ri0
                acc[2 * p + 1] += mr * ri0 + mi * rr2
        for p in range(n):
            sum_s[p, rws, re] = acc[2 * p]
            sum_s[p, rws, im] = acc[2 * p + 1]

    def backward_tile(rws):
        acc = [zero] * (2 * n)
        for k in range(n):
            rr, ri = resp_s[k, rws, re], resp_s[k, rws, im]
            ri0, rr2 = jnp.where(first, 0.0, ri), jnp.where(first, ri, rr)
            for r in range(n - k):
                gr, gi = gated_s[r + k, rws, re], gated_s[r + k, rws, im]
                acc[2 * r] += gr * rr + gi * ri0
                acc[2 * r + 1] += gi * rr2 - gr * ri0
        for r in range(n):
            sum_s[r, rws, re] = acc[2 * r]
            sum_s[r, rws, im] = acc[2 * r + 1]

        acc = [zero] * (2 * n)
        for r in range(n):
            mr, mi = mixed_s[r, rws, re], mixed_s[r, rws, im]
            mi0, mr2 = jnp.where(first, 0.0, mi), jnp.where(first, -mi, mr)
            for k in range(n - r):
                gr, gi = gated_s[r + k, rws, re], gated_s[r + k, rws, im]
                acc[2 * k] += mr * gr + mi0 * gi
                acc[2 * k + 1] += mi0 * gr - mr2 * gi
        for k in range(n):
            for c, at in ((0, re), (1, im)):
                own_sum = acc[2 * k + c]
                if k + 1 < n:
                    own_sum = own_sum + sign * acc[2 * k + 2 + c]
                sum_f[k, rws, at] = own_sum

    def result(half, a, sums, table, places, factor=None):
        block = jnp.concatenate([sums[places[p]].astype(bf16) for p in range(n)], axis=0)
        values = jnp.dot(block, table, preferred_element_type=f32)
        if factor is not None:
            values = values * factor
        send_out[half, :, a * part : (a + 1) * part, :] = values.astype(bf16).reshape(n, part, rows)

    def send_result(half, start, size, recv):
        rws = pl.ds(start, size)
        send_all(lambda peer: send_out.at[half, peer, rws], back.at[half, me, rws], back_send, recv)
        back[half, me, rws, :] = send_out[half, me, rws, :]

    def convolve(half, mixed_in, mixed_start, taps_in, recv):
        response(taps_in)
        mixed_s[...] = spectra(mixed_in, mixed_start, holder).reshape(n, part, 2 * rows)
        tiles(forward_tile)
        result(half, 0, sum_s, out_tab, order)
        send_result(half, 0, part, recv)

    def correlate(half, gated_in, start, recv):
        gated_s[...] = spectra(gated_in, start, holder).reshape(n, part, 2 * rows)
        tiles(backward_tile)
        result(half, 1, sum_s, out_tab, order)
        result(half, 2, sum_f, lag_tab, plain, scale)
        send_result(half, part, 2 * part, recv)

    wait_input(0)
    pass_on = pltpu.make_async_remote_copy(
        src_ref=recv_tm.at[:, pl.ds(0, part)], dst_ref=recv_t2,
        send_sem=pass_sem.at[0], recv_sem=pass_sem.at[1],
        device_id={"dp": 1 - core}, device_id_type=MESH,
    )
    pass_on.start()
    convolve(early, recv_tm, part, recv_tm, back_recv.at[0])
    wait_input(1)
    correlate(early, recv_g, 0, back_recv.at[0])
    pass_on.wait()
    wait_input(2)
    convolve(late, recv_m2, 0, recv_t2, back_recv.at[1])
    correlate(late, recv_m2, part, back_recv.at[1])

    landed = back.at[early, pl.ds(0, n - 1)]
    pltpu.make_async_copy(landed, landed, back_recv.at[0]).wait()
    for g in range(wide // 128):
        lanes = slice(g * 128, (g + 1) * 128)
        for i, value in enumerate(gated_group(back, early, g, q_ref, k_ref, v_ref, o_ref, gain_ref)):
            first_half[i, :, lanes] = value
    landed = back.at[late, pl.ds(0, n - 1)]
    pltpu.make_async_copy(landed, landed, back_recv.at[1]).wait()
    for _, _, _, recv in inputs:
        sent = recv.at[pl.ds(0, n - 1)]
        pltpu.make_async_copy(sent, sent, send_sem).wait()
    sent = send_out.at[:, pl.ds(0, n - 1)]
    pltpu.make_async_copy(sent, sent, back_send).wait()


def gate_kernel(
    back, first_half, q_ref, k_ref, v_ref, o_ref, gain_ref,
    hyena_hbm, gq_hbm, gk_hbm, gv_hbm, gf_hbm, second_half, sems,
):
    rows, channels = q_ref.shape
    wide = channels // HALVES
    early = lax.axis_index("dp")
    late = 1 - early
    outs = (hyena_hbm, gq_hbm, gk_hbm, gv_hbm, gf_hbm)
    stores = []

    def store(source, i, start, size, sem):
        stores.append(pltpu.make_async_copy(source, outs[i].at[:, pl.ds(pl.multiple_of(start, 128), size)], sem))
        stores[-1].start()

    for i in range(5):
        store(first_half.at[i], i, early * wide, wide, sems.at[0, i])
    for g in range(wide // 128):
        lanes = slice(g * 128, (g + 1) * 128)
        for i, value in enumerate(gated_group(back, late, g, q_ref, k_ref, v_ref, o_ref, gain_ref)):
            second_half[i, :, lanes] = value
            store(second_half.at[i, :, lanes], i, late * wide + g * 128, 128, sems.at[1 + g, i])
    for each in stores:
        each.wait()


def on_device(query_proj, key_proj, value_proj, filter_taps, skip_gain, out_grad, block_order):
    n = lax.axis_size("seq")
    rows, channels = query_proj.shape
    part = channels // n // HALVES
    bf16, f32 = jnp.bfloat16, jnp.float32
    vmem = pl.BlockSpec(memory_space=pltpu.VMEM)
    hbm = pl.BlockSpec(memory_space=pltpu.HBM)
    spec = pltpu.VMEM((n, part, 2 * rows), f32)
    small = pltpu.VMEM((n, part, rows), bf16)
    message = (HALVES, n, 3 * part, rows)
    block = jax.ShapeDtypeStruct((rows, channels), f32)
    tables = spectrum_tables(rows)
    kept = pl.pallas_call(
        functools.partial(exchange_kernel, n),
        out_shape=[
            jax.ShapeDtypeStruct(message, bf16),
            jax.ShapeDtypeStruct((5, rows, channels // HALVES), bf16),
            block, block, block, block,
            jax.ShapeDtypeStruct((1, channels), f32),
        ],
        in_specs=[hbm] * 8,
        out_specs=[vmem] * 7,
        scratch_shapes=[
            pltpu.VMEM((rows, channels), f32),
            pltpu.SMEM((n,), jnp.int32),
            pltpu.VMEM(tables.shape, bf16),
            pltpu.VMEM(message, bf16),
            pltpu.VMEM((n, 2 * part, rows), bf16),
            small, pltpu.VMEM((n, 2 * part, rows), bf16), small, small,
            pltpu.VMEM(message, bf16),
            spec, spec, spec, spec, spec,
            pltpu.SemaphoreType.DMA((8,)),
            pltpu.SemaphoreType.DMA(()),
            pltpu.SemaphoreType.DMA((4,)),
            pltpu.SemaphoreType.DMA((2,)),
            pltpu.SemaphoreType.DMA(()),
            pltpu.SemaphoreType.DMA((HALVES,)),
        ],
        compiler_params=pltpu.CompilerParams(
            collective_id=0, has_side_effects=True, vmem_limit_bytes=32 * 2**20
        ),
        name="exchange",
    )(*[
        pltpu.with_memory_space_constraint(x, pltpu.HBM)
        for x in (
            query_proj, key_proj, value_proj, out_grad, filter_taps, skip_gain[None, :], block_order,
            jnp.asarray(tables),
        )
    ])
    result = jax.ShapeDtypeStruct((rows, channels), bf16)
    return pl.pallas_call(
        gate_kernel,
        out_shape=[result] * 5,
        in_specs=[vmem] * 7,
        out_specs=[hbm] * 5,
        scratch_shapes=[
            pltpu.VMEM((5, rows, channels // HALVES), bf16),
            pltpu.SemaphoreType.DMA((1 + channels // HALVES // 128, 5)),
        ],
        compiler_params=pltpu.CompilerParams(vmem_limit_bytes=32 * 2**20),
        name="gate",
    )(*kept)


def solution(mesh):
    placed = (
        P(("dp", "seq"), "chan"),
        P(("dp", "seq"), "chan"),
        P(("dp", "seq"), "chan"),
        P("seq", "chan"),
        P("chan"),
        P(("dp", "seq"), "chan"),
        P("dp"),
    )
    return jax.shard_map(
        on_device,
        mesh=mesh,
        in_specs=placed,
        out_specs=(P(("dp", "seq"), "chan"),) * 5,
        check_vma=False,
    )
```

```python
import functools
import math

import jax
import jax.numpy as jnp
import ml_dtypes
import numpy as np
from jax import lax
from jax.experimental import pallas as pl
from jax.experimental.pallas import tpu as pltpu
from jax.sharding import PartitionSpec as P

MESH = pl.DeviceIdType.MESH
HALVES = 2


def spectrum_tables(rows):
    length = 2 * rows
    time = np.arange(rows)[:, None]
    freq = np.arange(rows)[None, :]
    angle = 2.0 * np.pi / length * ((time * freq) % length)
    middle = 1.0 - 2.0 * (time % 2)
    sine = np.where(freq == 0, middle, -np.sin(angle))
    forward = np.concatenate([np.cos(angle), sine], axis=1)
    sign = 1.0 - 2.0 * (freq % 2)
    weight = np.where(freq == 0, 1.0, 2.0) / length
    output = np.concatenate([weight * sign * np.cos(angle), weight * sign * sine], axis=1).T
    lag_sine = np.where(freq == 0, middle, np.sin(angle))
    lags = np.concatenate([weight * np.cos(angle), weight * lag_sine], axis=1).T
    stacked = np.concatenate([forward[:, :rows], forward[:, rows:], output, lags], axis=0)
    return stacked.astype(ml_dtypes.bfloat16)


def gated_group(back, half, g, q_ref, k_ref, v_ref, o_ref, gain_ref):
    part = back.shape[2] // 3
    wide = q_ref.shape[1] // HALVES
    bf16, f32 = jnp.bfloat16, jnp.float32
    turned = []
    for a in range(3):
        pieces = [back[half, g * (128 // part) + i, a * part : (a + 1) * part, :] for i in range(128 // part)]
        turned.append(jnp.concatenate(pieces, axis=0).astype(f32).T)
    lanes = pl.ds(pl.multiple_of(half * wide + g * 128, 128), 128)
    q, k, v, o = q_ref[:, lanes], k_ref[:, lanes], v_ref[:, lanes], o_ref[:, lanes]
    gain = gain_ref[:, lanes]
    conv_out = turned[0] + gain * (k * v).astype(bf16).astype(f32)
    conv_grad = turned[1] + gain * (o * q).astype(bf16).astype(f32)
    values = (q * conv_out, o * conv_out, conv_grad * v, conv_grad * k, turned[2])
    return [value.astype(bf16) for value in values]


def exchange_kernel(
    n, q_hbm, k_hbm, v_hbm, o_hbm, taps_hbm, gain_hbm, order_hbm, tables_hbm,
    back, first_half, q_ref, k_ref, v_ref, o_ref, gain_ref,
    taps_ref, order_ref, tables, send_in, recv_tm, recv_g, recv_m2, recv_g2, recv_t2, send_out,
    mixed_s, gated_s, resp_s, sum_s, sum_f,
    load_sem, send_sem, recv_sem, pass_sem, back_send, back_recv,
):
    me, core = lax.axis_index("seq"), lax.axis_index("dp")
    rows, channels = q_ref.shape
    own = channels // n
    part = own // HALVES
    wide = channels // HALVES
    scale = 1.0 / math.sqrt(rows * n)
    bf16, f32 = jnp.bfloat16, jnp.float32

    hops = [(h, z) for h in (1, 0) for z in (4, 3, 5, 2, 6, 1, 7, 0) if (h, z) != (0, 0)]
    ring = n // 2
    odd = lax.rem(me // ring, 2)
    peers = {
        (h, z): lax.rem(me // ring + h, 2) * ring + lax.rem(me + z + (ring - 2 * z) * odd, ring) for h, z in hops
    }

    barrier = pltpu.get_barrier_semaphore()
    for hop in sorted(hops, key=lambda hop: -2 * hop[0] - min(hop[1], ring - hop[1])):
        pl.semaphore_signal(barrier, inc=1, device_id={"seq": peers[hop]}, device_id_type=MESH)
    pl.semaphore_signal(barrier, inc=1, device_id={"dp": 1 - core}, device_id_type=MESH)

    loads = [
        pltpu.make_async_copy(src, dst, load_sem.at[i])
        for i, (src, dst) in enumerate((
            (taps_hbm, taps_ref), (k_hbm, k_ref), (v_hbm, v_ref), (o_hbm, o_ref), (q_hbm, q_ref),
            (tables_hbm, tables), (order_hbm, order_ref), (gain_hbm, gain_ref),
        ))
    ]
    for load in loads:
        load.start()

    def turn(a):
        for g in range(channels // 128):
            cols = slice(g * 128, (g + 1) * 128)
            if a == 0:
                block = taps_ref[:, cols] * scale
            elif a == 1:
                block = k_ref[:, cols] * v_ref[:, cols]
            else:
                block = o_ref[:, cols] * q_ref[:, cols]
            turned = block.T.astype(bf16)
            for i in range(128 // part):
                half, peer = divmod(g * (128 // part) + i, n)
                send_in[half, peer, a * part : (a + 1) * part, :] = turned[i * part : (i + 1) * part]


    def send_all(source, target, send, recv, group=None):
        for hop in group or hops:
            peer = peers[hop]
            pltpu.make_async_remote_copy(
                src_ref=source(peer), dst_ref=target, send_sem=send, recv_sem=recv,
                device_id={"seq": peer}, device_id_type=MESH,
            ).start()

    early, late = core, 1 - core
    inputs = (
        (early, 0, 2 * part, recv_tm), (early, 2 * part, part, recv_g),
        (late, part, 2 * part, recv_m2),
    )

    far = [(h, z) for h, z in hops if 2 * h + min(z, 8 - z) >= 5]
    near = [hop for hop in hops if hop not in far]

    def send_input(i, group=None):
        half, start, size, recv = inputs[i]
        rws = pl.ds(start, size)
        send_all(lambda peer: send_in.at[half, peer, rws], recv.at[me], send_sem, recv_sem.at[i], group)
        if group is not near:
            recv[me] = send_in[half, me, rws, :]

    def wait_input(i):
        landed = inputs[i][3].at[pl.ds(0, n - 1)]
        pltpu.make_async_copy(landed, landed, recv_sem.at[i]).wait()

    loads[0].wait()
    turn(0)
    loads[1].wait()
    loads[2].wait()
    turn(1)
    loads[3].wait()
    loads[4].wait()
    turn(2)
    pl.semaphore_wait(barrier, n)
    for group in (far, near):
        send_input(0, group)
        send_input(1, group)
    send_input(2)

    for load in loads[5:]:
        load.wait()
    fwd = jnp.concatenate([tables[0:rows], tables[rows : 2 * rows]], axis=1)
    out_tab, lag_tab = tables[2 * rows : 4 * rows], tables[4 * rows : 6 * rows]

    order = [order_ref[p] for p in range(n)]
    holder = []
    for j in range(n):
        at = jnp.int32(0)
        for p in range(1, n):
            at = jnp.where(order[p] == j, p, at)
        holder.append(at)
    plain = list(range(n))

    lane = lax.broadcasted_iota(jnp.int32, (8, 128), 1)
    first = lane == 0
    sign = jnp.where(lane % 2 == 0, 1.0, -1.0).astype(f32)
    wide_lane = lax.broadcasted_iota(jnp.int32, (n * part, 2 * rows), 1)
    wide_sign = jnp.where(wide_lane % 2 == 0, 1.0, -1.0).astype(f32)
    re, im = slice(0, 128), slice(128, 256)
    zero = jnp.zeros((8, 128), f32)

    def spectra(recv, start, places):
        block = jnp.concatenate([recv[places[j], start : start + part, :] for j in range(n)], axis=0)
        return jnp.dot(block, fwd, preferred_element_type=f32)

    def response(recv):
        taps_spec = spectra(recv, 0, plain)
        before = jnp.concatenate([jnp.zeros((part, 2 * rows), f32), taps_spec[: (n - 1) * part]], axis=0)
        resp_s[...] = (before + wide_sign * taps_spec).reshape(n, part, 2 * rows)

    def tiles(body):
        def step(u, _):
            body(pl.ds(pl.multiple_of(u * 8, 8), 8))
            return 0

        lax.fori_loop(0, part // 8, step, 0)

    def forward_tile(rws):
        acc = [zero] * (2 * n)
        for k in range(n):
            rr, ri = resp_s[k, rws, re], resp_s[k, rws, im]
            ri0, rr2 = jnp.where(first, 0.0, ri), jnp.where(first, ri, rr)
            for p in range(k, n):
                mr, mi = mixed_s[p - k, rws, re], mixed_s[p - k, rws, im]
                acc[2 * p] += mr * rr - mi * ri0
                acc[2 * p + 1] += mr * ri0 + mi * rr2
        for p in range(n):
            sum_s[p, rws, re] = acc[2 * p]
            sum_s[p, rws, im] = acc[2 * p + 1]

    def backward_tile(rws):
        acc = [zero] * (2 * n)
        for k in range(n):
            rr, ri = resp_s[k, rws, re], resp_s[k, rws, im]
            ri0, rr2 = jnp.where(first, 0.0, ri), jnp.where(first, ri, rr)
            for r in range(n - k):
                gr, gi = gated_s[r + k, rws, re], gated_s[r + k, rws, im]
                acc[2 * r] += gr * rr + gi * ri0
                acc[2 * r + 1] += gi * rr2 - gr * ri0
        for r in range(n):
            sum_s[r, rws, re] = acc[2 * r]
            sum_s[r, rws, im] = acc[2 * r + 1]

        acc = [zero] * (2 * n)
        for r in range(n):
            mr, mi = mixed_s[r, rws, re], mixed_s[r, rws, im]
            mi0, mr2 = jnp.where(first, 0.0, mi), jnp.where(first, -mi, mr)
            for k in range(n - r):
                gr, gi = gated_s[r + k, rws, re], gated_s[r + k, rws, im]
                acc[2 * k] += mr * gr + mi0 * gi
                acc[2 * k + 1] += mi0 * gr - mr2 * gi
        for k in range(n):
            for c, at in ((0, re), (1, im)):
                own_sum = acc[2 * k + c]
                if k + 1 < n:
                    own_sum = own_sum + sign * acc[2 * k + 2 + c]
                sum_f[k, rws, at] = own_sum

    def result(half, a, sums, table, places, factor=None):
        block = jnp.concatenate([sums[places[p]].astype(bf16) for p in range(n)], axis=0)
        values = jnp.dot(block, table, preferred_element_type=f32)
        if factor is not None:
            values = values * factor
        send_out[half, :, a * part : (a + 1) * part, :] = values.astype(bf16).reshape(n, part, rows)

    def send_result(half, start, size, recv):
        rws = pl.ds(start, size)
        send_all(lambda peer: send_out.at[half, peer, rws], back.at[half, me, rws], back_send, recv)
        back[half, me, rws, :] = send_out[half, me, rws, :]

    def convolve(half, mixed_in, mixed_start, taps_in, recv):
        response(taps_in)
        mixed_s[...] = spectra(mixed_in, mixed_start, holder).reshape(n, part, 2 * rows)
        tiles(forward_tile)
        result(half, 0, sum_s, out_tab, order)
        send_result(half, 0, part, recv)

    def correlate(half, gated_in, start, recv):
        gated_s[...] = spectra(gated_in, start, holder).reshape(n, part, 2 * rows)
        tiles(backward_tile)
        result(half, 1, sum_s, out_tab, order)
        result(half, 2, sum_f, lag_tab, plain, scale)
        send_result(half, part, 2 * part, recv)

    wait_input(0)
    pass_on = pltpu.make_async_remote_copy(
        src_ref=recv_tm.at[:, pl.ds(0, part)], dst_ref=recv_t2,
        send_sem=pass_sem.at[0], recv_sem=pass_sem.at[1],
        device_id={"dp": 1 - core}, device_id_type=MESH,
    )
    pass_on.start()
    convolve(early, recv_tm, part, recv_tm, back_recv.at[0])
    wait_input(1)
    correlate(early, recv_g, 0, back_recv.at[0])
    pass_on.wait()
    wait_input(2)
    convolve(late, recv_m2, 0, recv_t2, back_recv.at[1])
    correlate(late, recv_m2, part, back_recv.at[1])

    landed = back.at[early, pl.ds(0, n - 1)]
    pltpu.make_async_copy(landed, landed, back_recv.at[0]).wait()
    for g in range(wide // 128):
        lanes = slice(g * 128, (g + 1) * 128)
        for i, value in enumerate(gated_group(back, early, g, q_ref, k_ref, v_ref, o_ref, gain_ref)):
            first_half[i, :, lanes] = value
    landed = back.at[late, pl.ds(0, n - 1)]
    pltpu.make_async_copy(landed, landed, back_recv.at[1]).wait()
    for _, _, _, recv in inputs:
        sent = recv.at[pl.ds(0, n - 1)]
        pltpu.make_async_copy(sent, sent, send_sem).wait()
    sent = send_out.at[:, pl.ds(0, n - 1)]
    pltpu.make_async_copy(sent, sent, back_send).wait()


def gate_kernel(
    back, first_half, q_ref, k_ref, v_ref, o_ref, gain_ref,
    hyena_hbm, gq_hbm, gk_hbm, gv_hbm, gf_hbm, second_half, sems,
):
    rows, channels = q_ref.shape
    wide = channels // HALVES
    early = lax.axis_index("dp")
    late = 1 - early
    outs = (hyena_hbm, gq_hbm, gk_hbm, gv_hbm, gf_hbm)
    stores = []

    def store(source, i, start, size, sem):
        stores.append(pltpu.make_async_copy(source, outs[i].at[:, pl.ds(pl.multiple_of(start, 128), size)], sem))
        stores[-1].start()

    for i in range(5):
        store(first_half.at[i], i, early * wide, wide, sems.at[0, i])
    for g in range(wide // 128):
        lanes = slice(g * 128, (g + 1) * 128)
        for i, value in enumerate(gated_group(back, late, g, q_ref, k_ref, v_ref, o_ref, gain_ref)):
            second_half[i, :, lanes] = value
            store(second_half.at[i, :, lanes], i, late * wide + g * 128, 128, sems.at[1 + g, i])
    for each in stores:
        each.wait()


def on_device(query_proj, key_proj, value_proj, filter_taps, skip_gain, out_grad, block_order):
    n = lax.axis_size("seq")
    rows, channels = query_proj.shape
    part = channels // n // HALVES
    bf16, f32 = jnp.bfloat16, jnp.float32
    vmem = pl.BlockSpec(memory_space=pltpu.VMEM)
    hbm = pl.BlockSpec(memory_space=pltpu.HBM)
    spec = pltpu.VMEM((n, part, 2 * rows), f32)
    small = pltpu.VMEM((n, part, rows), bf16)
    message = (HALVES, n, 3 * part, rows)
    block = jax.ShapeDtypeStruct((rows, channels), f32)
    tables = spectrum_tables(rows)
    kept = pl.pallas_call(
        functools.partial(exchange_kernel, n),
        out_shape=[
            jax.ShapeDtypeStruct(message, bf16),
            jax.ShapeDtypeStruct((5, rows, channels // HALVES), bf16),
            block, block, block, block,
            jax.ShapeDtypeStruct((1, channels), f32),
        ],
        in_specs=[hbm] * 8,
        out_specs=[vmem] * 7,
        scratch_shapes=[
            pltpu.VMEM((rows, channels), f32),
            pltpu.SMEM((n,), jnp.int32),
            pltpu.VMEM(tables.shape, bf16),
            pltpu.VMEM(message, bf16),
            pltpu.VMEM((n, 2 * part, rows), bf16),
            small, pltpu.VMEM((n, 2 * part, rows), bf16), small, small,
            pltpu.VMEM(message, bf16),
            spec, spec, spec, spec, spec,
            pltpu.SemaphoreType.DMA((8,)),
            pltpu.SemaphoreType.DMA(()),
            pltpu.SemaphoreType.DMA((4,)),
            pltpu.SemaphoreType.DMA((2,)),
            pltpu.SemaphoreType.DMA(()),
            pltpu.SemaphoreType.DMA((HALVES,)),
        ],
        compiler_params=pltpu.CompilerParams(
            collective_id=0, has_side_effects=True, vmem_limit_bytes=32 * 2**20
        ),
        name="exchange",
    )(*[
        pltpu.with_memory_space_constraint(x, pltpu.HBM)
        for x in (
            query_proj, key_proj, value_proj, out_grad, filter_taps, skip_gain[None, :], block_order,
            jnp.asarray(tables),
        )
    ])
    result = jax.ShapeDtypeStruct((rows, channels), bf16)
    return pl.pallas_call(
        gate_kernel,
        out_shape=[result] * 5,
        in_specs=[vmem] * 7,
        out_specs=[hbm] * 5,
        scratch_shapes=[
            pltpu.VMEM((5, rows, channels // HALVES), bf16),
            pltpu.SemaphoreType.DMA((1 + channels // HALVES // 128, 5)),
        ],
        compiler_params=pltpu.CompilerParams(vmem_limit_bytes=32 * 2**20),
        name="gate",
    )(*kept)


def solution(mesh):
    placed = (
        P(("dp", "seq"), "chan"),
        P(("dp", "seq"), "chan"),
        P(("dp", "seq"), "chan"),
        P("seq", "chan"),
        P("chan"),
        P(("dp", "seq"), "chan"),
        P("dp"),
    )
    return jax.shard_map(
        on_device,
        mesh=mesh,
        in_specs=placed,
        out_specs=(P(("dp", "seq"), "chan"),) * 5,
        check_vma=False,
    )
```

```python
import functools
import math

import jax
import jax.numpy as jnp
import ml_dtypes
import numpy as np
from jax import lax
from jax.experimental import pallas as pl
from jax.experimental.pallas import tpu as pltpu
from jax.sharding import PartitionSpec as P

MESH = pl.DeviceIdType.MESH
HALVES = 2


def spectrum_tables(rows):
    length = 2 * rows
    time = np.arange(rows)[:, None]
    freq = np.arange(rows)[None, :]
    angle = 2.0 * np.pi / length * ((time * freq) % length)
    middle = 1.0 - 2.0 * (time % 2)
    sine = np.where(freq == 0, middle, -np.sin(angle))
    forward = np.concatenate([np.cos(angle), sine], axis=1)
    sign = 1.0 - 2.0 * (freq % 2)
    weight = np.where(freq == 0, 1.0, 2.0) / length
    output = np.concatenate([weight * sign * np.cos(angle), weight * sign * sine], axis=1).T
    lag_sine = np.where(freq == 0, middle, np.sin(angle))
    lags = np.concatenate([weight * np.cos(angle), weight * lag_sine], axis=1).T
    stacked = np.concatenate([forward[:, :rows], forward[:, rows:], output, lags], axis=0)
    return stacked.astype(ml_dtypes.bfloat16)


def gated_group(back, half, g, q_ref, k_ref, v_ref, o_ref, gain_ref):
    part = back.shape[2] // 3
    wide = q_ref.shape[1] // HALVES
    bf16, f32 = jnp.bfloat16, jnp.float32
    turned = []
    for a in range(3):
        pieces = [back[half, g * (128 // part) + i, a * part : (a + 1) * part, :] for i in range(128 // part)]
        turned.append(jnp.concatenate(pieces, axis=0).astype(f32).T)
    lanes = pl.ds(pl.multiple_of(half * wide + g * 128, 128), 128)
    q, k, v, o = q_ref[:, lanes], k_ref[:, lanes], v_ref[:, lanes], o_ref[:, lanes]
    gain = gain_ref[:, lanes]
    conv_out = turned[0] + gain * (k * v).astype(bf16).astype(f32)
    conv_grad = turned[1] + gain * (o * q).astype(bf16).astype(f32)
    values = (q * conv_out, o * conv_out, conv_grad * v, conv_grad * k, turned[2])
    return [value.astype(bf16) for value in values]


def exchange_kernel(
    n, q_hbm, k_hbm, v_hbm, o_hbm, taps_hbm, gain_hbm, order_hbm, tables_hbm,
    back, first_half, q_ref, k_ref, v_ref, o_ref, gain_ref,
    taps_ref, order_ref, tables, send_in, recv_tm, recv_g, recv_m2, recv_g2, recv_t2, send_out,
    mixed_s, gated_s, resp_s, sum_s, sum_f,
    load_sem, send_sem, recv_sem, pass_sem, back_send, back_recv,
):
    me, core = lax.axis_index("seq"), lax.axis_index("dp")
    rows, channels = q_ref.shape
    own = channels // n
    part = own // HALVES
    wide = channels // HALVES
    scale = 1.0 / math.sqrt(rows * n)
    bf16, f32 = jnp.bfloat16, jnp.float32

    hops = [(h, z) for h in (1, 0) for z in (4, 3, 5, 2, 6, 1, 7, 0) if (h, z) != (0, 0)]
    ring = n // 2
    odd = lax.rem(me // ring, 2)
    peers = {
        (h, z): lax.rem(me // ring + h, 2) * ring + lax.rem(me + z + (ring - 2 * z) * odd, ring) for h, z in hops
    }

    barrier = pltpu.get_barrier_semaphore()
    for hop in sorted(hops, key=lambda hop: -2 * hop[0] - min(hop[1], ring - hop[1])):
        pl.semaphore_signal(barrier, inc=1, device_id={"seq": peers[hop]}, device_id_type=MESH)
    pl.semaphore_signal(barrier, inc=1, device_id={"dp": 1 - core}, device_id_type=MESH)

    loads = [
        pltpu.make_async_copy(src, dst, load_sem.at[i])
        for i, (src, dst) in enumerate((
            (taps_hbm, taps_ref), (k_hbm, k_ref), (v_hbm, v_ref), (o_hbm, o_ref), (q_hbm, q_ref),
            (tables_hbm, tables), (order_hbm, order_ref), (gain_hbm, gain_ref),
        ))
    ]
    for load in loads:
        load.start()

    def turn(a):
        for g in range(channels // 128):
            cols = slice(g * 128, (g + 1) * 128)
            if a == 0:
                block = taps_ref[:, cols] * scale
            elif a == 1:
                block = k_ref[:, cols] * v_ref[:, cols]
            else:
                block = o_ref[:, cols] * q_ref[:, cols]
            turned = block.T.astype(bf16)
            for i in range(128 // part):
                half, peer = divmod(g * (128 // part) + i, n)
                send_in[half, peer, a * part : (a + 1) * part, :] = turned[i * part : (i + 1) * part]


    def send_all(source, target, send, recv, group=None):
        for hop in group or hops:
            peer = peers[hop]
            pltpu.make_async_remote_copy(
                src_ref=source(peer), dst_ref=target, send_sem=send, recv_sem=recv,
                device_id={"seq": peer}, device_id_type=MESH,
            ).start()

    early, late = core, 1 - core
    inputs = (
        (early, 0, 2 * part, recv_tm), (early, 2 * part, part, recv_g),
        (late, part, 2 * part, recv_m2),
    )

    far = [(h, z) for h, z in hops if 2 * h + min(z, 8 - z) >= 5]
    near = [hop for hop in hops if hop not in far]

    partner_first = sorted(hops, key=lambda hop: hop != (1, 0))

    def send_input(i, group=None):
        half, start, size, recv = inputs[i]
        rws = pl.ds(start, size)
        send_all(lambda peer: send_in.at[half, peer, rws], recv.at[me], send_sem, recv_sem.at[i], group)
        if group is not near:
            recv[me] = send_in[half, me, rws, :]

    def wait_input(i):
        landed = inputs[i][3].at[pl.ds(0, n - 1)]
        pltpu.make_async_copy(landed, landed, recv_sem.at[i]).wait()

    loads[0].wait()
    turn(0)
    loads[1].wait()
    loads[2].wait()
    turn(1)
    loads[3].wait()
    loads[4].wait()
    turn(2)
    pl.semaphore_wait(barrier, n)
    for group in (far, near):
        send_input(0, group)
        send_input(1, group)
    send_input(2)

    for load in loads[5:]:
        load.wait()
    fwd = jnp.concatenate([tables[0:rows], tables[rows : 2 * rows]], axis=1)
    out_tab, lag_tab = tables[2 * rows : 4 * rows], tables[4 * rows : 6 * rows]

    order = [order_ref[p] for p in range(n)]
    holder = []
    for j in range(n):
        at = jnp.int32(0)
        for p in range(1, n):
            at = jnp.where(order[p] == j, p, at)
        holder.append(at)
    plain = list(range(n))

    lane = lax.broadcasted_iota(jnp.int32, (8, 128), 1)
    first = lane == 0
    sign = jnp.where(lane % 2 == 0, 1.0, -1.0).astype(f32)
    wide_lane = lax.broadcasted_iota(jnp.int32, (n * part, 2 * rows), 1)
    wide_sign = jnp.where(wide_lane % 2 == 0, 1.0, -1.0).astype(f32)
    re, im = slice(0, 128), slice(128, 256)
    zero = jnp.zeros((8, 128), f32)

    def spectra(recv, start, places):
        block = jnp.concatenate([recv[places[j], start : start + part, :] for j in range(n)], axis=0)
        return jnp.dot(block, fwd, preferred_element_type=f32)

    def response(recv):
        taps_spec = spectra(recv, 0, plain)
        before = jnp.concatenate([jnp.zeros((part, 2 * rows), f32), taps_spec[: (n - 1) * part]], axis=0)
        resp_s[...] = (before + wide_sign * taps_spec).reshape(n, part, 2 * rows)

    def tiles(body):
        def step(u, _):
            body(pl.ds(pl.multiple_of(u * 8, 8), 8))
            return 0

        lax.fori_loop(0, part // 8, step, 0)

    def forward_tile(rws):
        acc = [zero] * (2 * n)
        for k in range(n):
            rr, ri = resp_s[k, rws, re], resp_s[k, rws, im]
            ri0, rr2 = jnp.where(first, 0.0, ri), jnp.where(first, ri, rr)
            for p in range(k, n):
                mr, mi = mixed_s[p - k, rws, re], mixed_s[p - k, rws, im]
                acc[2 * p] += mr * rr - mi * ri0
                acc[2 * p + 1] += mr * ri0 + mi * rr2
        for p in range(n):
            sum_s[p, rws, re] = acc[2 * p]
            sum_s[p, rws, im] = acc[2 * p + 1]

    def backward_tile(rws):
        acc = [zero] * (2 * n)
        for k in range(n):
            rr, ri = resp_s[k, rws, re], resp_s[k, rws, im]
            ri0, rr2 = jnp.where(first, 0.0, ri), jnp.where(first, ri, rr)
            for r in range(n - k):
                gr, gi = gated_s[r + k, rws, re], gated_s[r + k, rws, im]
                acc[2 * r] += gr * rr + gi * ri0
                acc[2 * r + 1] += gi * rr2 - gr * ri0
        for r in range(n):
            sum_s[r, rws, re] = acc[2 * r]
            sum_s[r, rws, im] = acc[2 * r + 1]

        acc = [zero] * (2 * n)
        for r in range(n):
            mr, mi = mixed_s[r, rws, re], mixed_s[r, rws, im]
            mi0, mr2 = jnp.where(first, 0.0, mi), jnp.where(first, -mi, mr)
            for k in range(n - r):
                gr, gi = gated_s[r + k, rws, re], gated_s[r + k, rws, im]
                acc[2 * k] += mr * gr + mi0 * gi
                acc[2 * k + 1] += mi0 * gr - mr2 * gi
        for k in range(n):
            for c, at in ((0, re), (1, im)):
                own_sum = acc[2 * k + c]
                if k + 1 < n:
                    own_sum = own_sum + sign * acc[2 * k + 2 + c]
                sum_f[k, rws, at] = own_sum

    def result(half, a, sums, table, places, factor=None):
        block = jnp.concatenate([sums[places[p]].astype(bf16) for p in range(n)], axis=0)
        values = jnp.dot(block, table, preferred_element_type=f32)
        if factor is not None:
            values = values * factor
        send_out[half, :, a * part : (a + 1) * part, :] = values.astype(bf16).reshape(n, part, rows)

    def send_result(half, start, size, recv):
        rws = pl.ds(start, size)
        send_all(lambda peer: send_out.at[half, peer, rws], back.at[half, me, rws], back_send, recv, partner_first)
        back[half, me, rws, :] = send_out[half, me, rws, :]

    def convolve(half, mixed_in, mixed_start, taps_in, recv):
        response(taps_in)
        mixed_s[...] = spectra(mixed_in, mixed_start, holder).reshape(n, part, 2 * rows)
        tiles(forward_tile)
        result(half, 0, sum_s, out_tab, order)
        send_result(half, 0, part, recv)

    def correlate(half, gated_in, start, recv):
        gated_s[...] = spectra(gated_in, start, holder).reshape(n, part, 2 * rows)
        tiles(backward_tile)
        result(half, 1, sum_s, out_tab, order)
        result(half, 2, sum_f, lag_tab, plain, scale)
        send_result(half, part, 2 * part, recv)

    wait_input(0)
    pass_on = pltpu.make_async_remote_copy(
        src_ref=recv_tm.at[:, pl.ds(0, part)], dst_ref=recv_t2,
        send_sem=pass_sem.at[0], recv_sem=pass_sem.at[1],
        device_id={"dp": 1 - core}, device_id_type=MESH,
    )
    pass_on.start()
    convolve(early, recv_tm, part, recv_tm, back_recv.at[0])
    wait_input(1)
    correlate(early, recv_g, 0, back_recv.at[0])
    pass_on.wait()
    wait_input(2)
    convolve(late, recv_m2, 0, recv_t2, back_recv.at[1])
    correlate(late, recv_m2, part, back_recv.at[1])

    landed = back.at[early, pl.ds(0, n - 1)]
    pltpu.make_async_copy(landed, landed, back_recv.at[0]).wait()
    for g in range(wide // 128):
        lanes = slice(g * 128, (g + 1) * 128)
        for i, value in enumerate(gated_group(back, early, g, q_ref, k_ref, v_ref, o_ref, gain_ref)):
            first_half[i, :, lanes] = value
    landed = back.at[late, pl.ds(0, n - 1)]
    pltpu.make_async_copy(landed, landed, back_recv.at[1]).wait()
    for _, _, _, recv in inputs:
        sent = recv.at[pl.ds(0, n - 1)]
        pltpu.make_async_copy(sent, sent, send_sem).wait()
    sent = send_out.at[:, pl.ds(0, n - 1)]
    pltpu.make_async_copy(sent, sent, back_send).wait()


def gate_kernel(
    back, first_half, q_ref, k_ref, v_ref, o_ref, gain_ref,
    hyena_hbm, gq_hbm, gk_hbm, gv_hbm, gf_hbm, second_half, sems,
):
    rows, channels = q_ref.shape
    wide = channels // HALVES
    early = lax.axis_index("dp")
    late = 1 - early
    outs = (hyena_hbm, gq_hbm, gk_hbm, gv_hbm, gf_hbm)
    stores = []

    def store(source, i, start, size, sem):
        stores.append(pltpu.make_async_copy(source, outs[i].at[:, pl.ds(pl.multiple_of(start, 128), size)], sem))
        stores[-1].start()

    for i in range(5):
        store(first_half.at[i], i, early * wide, wide, sems.at[0, i])
    for g in range(wide // 128):
        lanes = slice(g * 128, (g + 1) * 128)
        for i, value in enumerate(gated_group(back, late, g, q_ref, k_ref, v_ref, o_ref, gain_ref)):
            second_half[i, :, lanes] = value
            store(second_half.at[i, :, lanes], i, late * wide + g * 128, 128, sems.at[1 + g, i])
    for each in stores:
        each.wait()


def on_device(query_proj, key_proj, value_proj, filter_taps, skip_gain, out_grad, block_order):
    n = lax.axis_size("seq")
    rows, channels = query_proj.shape
    part = channels // n // HALVES
    bf16, f32 = jnp.bfloat16, jnp.float32
    vmem = pl.BlockSpec(memory_space=pltpu.VMEM)
    hbm = pl.BlockSpec(memory_space=pltpu.HBM)
    spec = pltpu.VMEM((n, part, 2 * rows), f32)
    small = pltpu.VMEM((n, part, rows), bf16)
    message = (HALVES, n, 3 * part, rows)
    block = jax.ShapeDtypeStruct((rows, channels), f32)
    tables = spectrum_tables(rows)
    kept = pl.pallas_call(
        functools.partial(exchange_kernel, n),
        out_shape=[
            jax.ShapeDtypeStruct(message, bf16),
            jax.ShapeDtypeStruct((5, rows, channels // HALVES), bf16),
            block, block, block, block,
            jax.ShapeDtypeStruct((1, channels), f32),
        ],
        in_specs=[hbm] * 8,
        out_specs=[vmem] * 7,
        scratch_shapes=[
            pltpu.VMEM((rows, channels), f32),
            pltpu.SMEM((n,), jnp.int32),
            pltpu.VMEM(tables.shape, bf16),
            pltpu.VMEM(message, bf16),
            pltpu.VMEM((n, 2 * part, rows), bf16),
            small, pltpu.VMEM((n, 2 * part, rows), bf16), small, small,
            pltpu.VMEM(message, bf16),
            spec, spec, spec, spec, spec,
            pltpu.SemaphoreType.DMA((8,)),
            pltpu.SemaphoreType.DMA(()),
            pltpu.SemaphoreType.DMA((4,)),
            pltpu.SemaphoreType.DMA((2,)),
            pltpu.SemaphoreType.DMA(()),
            pltpu.SemaphoreType.DMA((HALVES,)),
        ],
        compiler_params=pltpu.CompilerParams(
            collective_id=0, has_side_effects=True, vmem_limit_bytes=32 * 2**20
        ),
        name="exchange",
    )(*[
        pltpu.with_memory_space_constraint(x, pltpu.HBM)
        for x in (
            query_proj, key_proj, value_proj, out_grad, filter_taps, skip_gain[None, :], block_order,
            jnp.asarray(tables),
        )
    ])
    result = jax.ShapeDtypeStruct((rows, channels), bf16)
    return pl.pallas_call(
        gate_kernel,
        out_shape=[result] * 5,
        in_specs=[vmem] * 7,
        out_specs=[hbm] * 5,
        scratch_shapes=[
            pltpu.VMEM((5, rows, channels // HALVES), bf16),
            pltpu.SemaphoreType.DMA((1 + channels // HALVES // 128, 5)),
        ],
        compiler_params=pltpu.CompilerParams(vmem_limit_bytes=32 * 2**20),
        name="gate",
    )(*kept)


def solution(mesh):
    placed = (
        P(("dp", "seq"), "chan"),
        P(("dp", "seq"), "chan"),
        P(("dp", "seq"), "chan"),
        P("seq", "chan"),
        P("chan"),
        P(("dp", "seq"), "chan"),
        P("dp"),
    )
    return jax.shard_map(
        on_device,
        mesh=mesh,
        in_specs=placed,
        out_specs=(P(("dp", "seq"), "chan"),) * 5,
        check_vma=False,
    )
```
